256 devices in a mesh: outer: 4 (over y), inner: 64 (over z, x, core).
Axes of the slice: x: 4, y: 4, z: 8, core: 2. Of those that a mesh axis runs over, the one named last changes fastest.
Arguments:
- inputs: bfloat16 [2, 16384, 4096], P(None, ('outer', 'inner')), may hold values from -6 to 6
- grad_out: bfloat16 [2, 16384, 4096], P(None, ('outer', 'inner')), may hold values from -6 to 6
- gate_weights: bfloat16 [2, 16, 256, 256], replicated, may hold values from -0.375 to 0.375
- gate_biases: float32 [2, 4096], replicated, may hold values from -4 to 4
- decay_rate: float32 [4096], replicated, may hold values from 1.2207031e-06 to 0.00833333333, as said below
Outputs:
- input_grad: bfloat16 [2, 16384, 4096], P(None, ('outer', 'inner'))
- gate_grads: float32 [8192, 256], P(('outer', 'inner'))
- bias_grads: float32 [2, 4096], replicated
- rate_grad: float32 [4096], replicated
The draws below stay inside these ranges and needn't reach their ends.
Inputs may be any that keep to these rules, and one draw needn't show every extreme that they name: `decay_rate`: positive per-channel rates.
All inputs are finite; a program needn't handle non-finite values.
Results may differ from the reference program's by a relative error of at most 0.0025.
Values sent between devices are 32-bit elements; how exact they have to be, the bound alone decides.
A program may use at most 128 MiB of HBM per device.

```python
import jax
import jax.numpy as jnp
from jax import lax

BLOCKS = 16
BW = 256
D = 4096
SEQS = 2
STEPS_DEV = 64
SEQ_LEN = 16384


def draw_decay_rate(key, part):
    key = jax.random.fold_in(key, 7)
    key_pick, key_slow, key_fast = jax.random.split(key, 3)
    slow_share = 0.5
    is_slow = jax.random.uniform(key_pick, (D,), jnp.float32) < slow_share
    slow_rate = jnp.exp(jax.random.uniform(key_slow, (D,), jnp.float32, jnp.log(0.02), jnp.log(0.5))) / SEQ_LEN
    fast_rate = jnp.exp(jax.random.uniform(key_fast, (D,), jnp.float32, jnp.log(1.0 / 200), jnp.log(1.0 / 120)))
    return jnp.where(is_slow, slow_rate, fast_rate).astype(jnp.float32)


def shard_levels(own_key, extent, shards, least, largest):
    level, own = 1.0, jax.random.fold_in(own_key, 6)
    for position, parts in shards:
        steps = jnp.exp(jax.random.uniform(jax.random.fold_in(own, position), (parts,), jnp.float32, least / len(shards), largest / len(shards)))
        level = level * jnp.repeat(steps, extent[position] // parts).reshape([-1 if axis == position else 1 for axis in range(len(extent))])
    return level


def scatter_about(stream_key, extent, spread, limit, cuts=(), held_as=jnp.bfloat16):
    values = jax.random.normal(stream_key, extent, jnp.float32) * spread
    if len(cuts) > 0:
        values = shard_levels(stream_key, extent, cuts, -0.22, 0.18) * values
    return jnp.clip(values, min=-limit, max=limit).astype(held_as)


def setup_inputs(seed: int = 0) -> dict:
    key_list = jax.random.split(jax.random.key(seed), 6)
    inputs = scatter_about(key_list[0], (SEQS, SEQ_LEN, D), 1.0, 6.0, ((1, 256),))
    grad_out = scatter_about(key_list[1], (SEQS, SEQ_LEN, D), 1.0, 6.0, ((1, 256),))
    gate_weights = scatter_about(key_list[2], (2, BLOCKS, BW, BW), BW ** -0.5, 0.375)
    gate_biases = scatter_about(key_list[3], (2, D), 1.0, 4.0, (), jnp.float32)
    decay_rate = draw_decay_rate(jax.random.fold_in(key_list[5], 71), 0)
    return {"inputs": inputs, "grad_out": grad_out, "gate_weights": gate_weights, "gate_biases": gate_biases, "decay_rate": decay_rate}


rate_gain = 8.0

def gate_terms(block_in, gate_weights, gate_biases, decay_rate):
    seq_count, step_count, channels = block_in.shape
    blocks = gate_weights.shape[1]
    block_width = gate_weights.shape[2]
    pieces = block_in.reshape(seq_count * step_count, blocks, block_width)
    preacts = jnp.einsum('nkc,gkce->gnke', pieces.astype(jnp.float32), gate_weights.astype(jnp.float32))
    preacts = preacts.reshape(2, seq_count, step_count, channels) + gate_biases[:, None, None, :]
    recurrence = jax.nn.sigmoid(preacts[0])
    inject = jax.nn.sigmoid(preacts[1])
    values = block_in.astype(jnp.float32)
    log_decay = -rate_gain * recurrence * decay_rate
    decays = jnp.exp(log_decay)
    scales = jnp.sqrt(-jnp.expm1(2.0 * log_decay))
    driven = inject * values
    return (recurrence, inject, decays, scales, driven, values)

def gradients(block_in, previous, adjoint, gate_weights, decay_rate, terms):
    recurrence, inject, decays, scales, driven, values = terms
    seq_count, step_count, channels = block_in.shape
    blocks = gate_weights.shape[1]
    block_width = gate_weights.shape[2]
    driven_grad = adjoint * scales
    sensitive = rate_gain * (adjoint * driven * decays * decays / scales - adjoint * previous * decays)
    pre_recur = decay_rate * sensitive * recurrence * (1.0 - recurrence)
    pre_inject = driven_grad * values * inject * (1.0 - inject)
    rate_part = lax.optimization_barrier(jnp.sum(recurrence * sensitive, axis=(0, 1)))
    bias_part = jnp.stack([lax.optimization_barrier(jnp.sum(pre_recur, axis=(0, 1))), lax.optimization_barrier(jnp.sum(pre_inject, axis=(0, 1)))])
    pre_grads = jnp.stack([pre_recur, pre_inject]).astype(jnp.bfloat16)
    pre_grads = pre_grads.reshape(2, seq_count * step_count, blocks, block_width)
    through = jnp.einsum('gnke,gkce->nkc', pre_grads.astype(jnp.float32), gate_weights.astype(jnp.float32))
    input_grad = (driven_grad * inject + through.reshape(seq_count, step_count, channels)).astype(jnp.bfloat16)
    pieces = block_in.reshape(seq_count * step_count, blocks, block_width)
    weight_part = jnp.einsum('nkc,gnke->gkce', pieces.astype(jnp.float32), pre_grads.astype(jnp.float32))
    return (input_grad, weight_part.reshape(2 * blocks * block_width, block_width), bias_part, rate_part)

def reference(inputs, grad_out, gate_weights, gate_biases, decay_rate):
    block_count = SEQ_LEN // STEPS_DEV
    indices = jnp.arange(block_count, dtype=jnp.int32)

    def take(array, index):
        return lax.dynamic_slice_in_dim(array, index * STEPS_DEV, STEPS_DEV, 1)

    def advance(carried, element):
        return (element[0] * carried + element[1], carried)

    def forward_block(carried, index):
        terms = gate_terms(take(inputs, index), gate_weights, gate_biases, decay_rate)
        decays, scales, driven = (terms[2], terms[3], terms[4])
        ending, unused = lax.scan(advance, carried, (jnp.moveaxis(decays, 1, 0), jnp.moveaxis(scales * driven, 1, 0)))
        return (ending, carried)
    first_state = jnp.zeros((SEQS, D), jnp.float32)
    unused_end, starts = lax.scan(forward_block, first_state, indices)

    def retreat(incoming, element):
        adjoint = element[1] + incoming
        return (element[0] * adjoint, adjoint)

    def backward_block(carried, index):
        arriving, weight_sum, bias_sum, rate_sum = carried
        block_in = take(inputs, index)
        upstream = take(grad_out, index).astype(jnp.float32)
        terms = gate_terms(block_in, gate_weights, gate_biases, decay_rate)
        decays, scales, driven = (terms[2], terms[3], terms[4])
        unused_state, previous = lax.scan(advance, starts[index], (jnp.moveaxis(decays, 1, 0), jnp.moveaxis(scales * driven, 1, 0)))
        outgoing, adjoint = lax.scan(retreat, arriving, (jnp.moveaxis(decays, 1, 0), jnp.moveaxis(upstream, 1, 0)), reverse=True)
        previous = jnp.moveaxis(previous, 0, 1)
        adjoint = jnp.moveaxis(adjoint, 0, 1)
        input_grad, weight_part, bias_part, rate_part = gradients(block_in, previous, adjoint, gate_weights, decay_rate, terms)
        return ((outgoing, weight_sum + weight_part, bias_sum + bias_part, rate_sum + rate_part), input_grad)
    initial = (jnp.zeros((SEQS, D), jnp.float32), jnp.zeros((2 * BLOCKS * BW, BW), jnp.float32), jnp.zeros((2, D), jnp.float32), jnp.zeros((D,), jnp.float32))
    totals, grads = lax.scan(backward_block, initial, indices, reverse=True)
    input_grad = jnp.moveaxis(grads, 0, 1).reshape(SEQS, SEQ_LEN, D)
    return (input_grad, totals[1], totals[2], totals[3])
```

```python
import functools

import jax
import jax.numpy as jnp
from jax import lax
from jax.experimental import pallas as pl
from jax.experimental.pallas import tpu as pltpu
from jax.sharding import PartitionSpec as P

F32, BF16 = jnp.float32, jnp.bfloat16
rate_gain = 8.0
NY, NZ, NX, NC = 4, 8, 4, 2
GROUP = NX * NC
BLOCKS, BW, D = 16, 256, 4096
SEQS, STEPS = 2, 64
ROWS = SEQS * STEPS
PAIRS = BLOCKS // 2
SLAB = 32
SIZES = {"y": NY, "z": NZ, "x": NX}

PARTS = (
    ((0, 24), (0, 128), "xyz"),
    ((0, 24), (128, 128), "yzx"),
    ((24, 8), (0, 256), "zxy"),
)


def rounds_of(order):
    return [
        (stage, axis, step)
        for stage, axis in enumerate(order)
        for step in range(1, SIZES[axis] // 2 + 1)
    ]


ROUNDS = len(rounds_of("xyz"))


def free_axes(order, stage):
    return [axis for axis in "yzx" if axis in order[stage + 1 :]]


def lead_shape(axes, halved):
    shape = []
    for position, axis in enumerate(axes):
        half = halved and position == 0
        if axis == "y":
            shape += [1 if half else 2, 2]
        else:
            shape += [SIZES[axis] // 2 if half else SIZES[axis]]
    return tuple(shape)


def ring_buffers():
    shapes = []
    for (_, rows), (_, cols), order in PARTS:
        for stage, axis, step in rounds_of(order):
            axes = free_axes(order, stage)
            shapes.append((2,) + lead_shape(axes, step == 1) + (rows, cols))
    return shapes


RING_BUFFERS = ring_buffers()

EVENTS = [
    (2, 0), (0, 0), (1, 0), (2, 1), (2, 2), (0, 1), (1, 1), (2, 3),
    (0, 2), (1, 2), (2, 4), (0, 3), (1, 3), (2, 5), (0, 4), (1, 4), (2, 6),
    (0, 5), (1, 5), (2, 7), (0, 6), (1, 6), (0, 7), (1, 7),
]


def kernel(
    x_hbm, go_hbm, w_hbm, bias_hbm, rate_hbm,
    out_hbm, gg_ref, bg_ref, rg_ref,
    x_v, go_v, w_v, bias_v, rate_v, out_v,
    tri_v, pre_v, ld_v, drive_v, lc_v, split_v, dg_v, p_v,
    inv_v, pex_v, before_v, tail_v, c_v, e_v, f_v, q3_v, q4_v,
    sum_s, sum_r, zsum_r, ysum_r, ent_s, ent_r,
    vec_s, vec_r, vecz_r, vecy_r, veco_r,
    grad_v, part_v,
    in_sem, small_sem, out_sem,
    g1_send, g1_recv, z1_send, z1_recv, y1_send, y1_recv, g2_send, g2_recv,
    v1_send, v1_recv, vz_send, vz_recv, vy_send, vy_recv, v2_send, v2_recv,
    core_send, core_recv, ring_send, ring_recv,
    *ring_bufs,
):
    y = lax.axis_index("outer")
    inner = lax.axis_index("inner")
    z = inner // GROUP
    member = lax.rem(inner, GROUP)
    x = member // NC
    core = lax.rem(member, NC)

    def device(y_at, z_at, member_at):
        return (y_at, z_at * GROUP + member_at)

    barrier = pltpu.get_barrier_semaphore()

    def greet(target):
        pl.semaphore_signal(barrier, inc=1, device_id=target, device_id_type=pl.DeviceIdType.MESH)

    for step in range(1, GROUP):
        greet(device(y, z, lax.rem(member + step, GROUP)))
    for step in range(1, NZ):
        greet(device(y, lax.rem(z + step, NZ), member))
    for step in range(1, NY):
        greet(device(lax.rem(y + step, NY), z, member))

    def load_copies(k):
        lanes = pl.ds(pl.multiple_of(k * BW, BW), BW)
        return (
            pltpu.make_async_copy(x_hbm.at[:, lanes], x_v.at[k], in_sem.at[0, k]),
            pltpu.make_async_copy(w_hbm.at[:, k], w_v.at[:, k], in_sem.at[1, k]),
            pltpu.make_async_copy(go_hbm.at[:, lanes], go_v.at[k], in_sem.at[2, k]),
        )

    bias_copy = pltpu.make_async_copy(bias_hbm, bias_v, small_sem.at[0])
    rate_copy = pltpu.make_async_copy(rate_hbm, rate_v, small_sem.at[1])
    bias_copy.start()
    rate_copy.start()

    def start_loads(k, carry):
        for copy in load_copies(k):
            copy.start()
        return carry

    lax.fori_loop(0, BLOCKS, start_loads, 0)

    row = lax.broadcasted_iota(jnp.int32, (ROWS, 2 * ROWS), 0)
    col = lax.broadcasted_iota(jnp.int32, (ROWS, 2 * ROWS), 1)
    col = jnp.where(col >= ROWS, col - ROWS, col)
    same = jnp.where(row >= STEPS, 1, 0) == jnp.where(col >= STEPS, 1, 0)
    tri_v[0] = jnp.where(same & (col <= row), 1.0, 0.0).astype(BF16)
    tri_v[1] = jnp.where(same & (col < row), 1.0, 0.0).astype(BF16)
    tri_v[2] = jnp.where(same & (col >= row), 1.0, 0.0).astype(BF16)

    vec_s[...] = jnp.zeros_like(vec_s)
    bias_copy.wait()
    rate_copy.wait()

    def slabs():
        for j in range(2):
            for top in range(0, ROWS, SLAB):
                yield pl.ds(top, SLAB), pl.ds(j * 128, 128), j

    def split_store(b, which, top, lanes, value):
        high = value.astype(BF16)
        split_v[b, which, pl.ds(top, SLAB), lanes] = high
        split_v[b, which, pl.ds(ROWS + top, SLAB), lanes] = (value - high.astype(F32)).astype(BF16)

    def local_pair(pair, carry):
        for b in range(2):
            k = 2 * pair + b
            for copy in load_copies(k):
                copy.wait()
            xk = x_v[k]
            for g in range(2):
                pre_v[b, g] = jnp.dot(xk, w_v[g, k], preferred_element_type=F32)
        for b in range(2):
            k = 2 * pair + b
            for rows, lanes, j in slabs():
                column = pl.ds(pl.multiple_of(k * BW + j * 128, 128), 128)
                rate = rate_v[0:1, column]
                pre_r = pre_v[b, 0, rows, lanes] + bias_v[0:1, column]
                pre_i = pre_v[b, 1, rows, lanes] + bias_v[1:2, column]
                recur = 1.0 / (1.0 + jnp.exp(-pre_r))
                inject = 1.0 / (1.0 + jnp.exp(-pre_i))
                values = x_v[k, rows, lanes].astype(F32)
                log_decay = (-rate_gain * rate) * recur
                decay = jnp.exp(log_decay)
                series = -log_decay * (
                    1.0 + log_decay * (0.5 + log_decay * (1.0 / 6.0 + log_decay * (1.0 / 24.0)))
                )
                lost = jnp.where(log_decay > -0.1, series, 1.0 - decay)
                square = lost * (1.0 + decay)
                inverse_scale = lax.rsqrt(square)
                scale = square * inverse_scale
                driven = inject * values
                drive_v[b, rows, lanes] = scale * driven
                ld_v[b, rows, lanes] = log_decay
                split_store(b, 0, rows.start, lanes, log_decay)
                gained = rate_gain * recur
                e = gained * decay
                e_v[k, rows, lanes] = e
                c_v[k, rows, lanes] = e * decay * driven * inverse_scale
                f_v[k, rows, lanes] = rate * (1.0 - recur)
                q4 = scale * inject
                q4_v[k, rows, lanes] = q4
                q3_v[k, rows, lanes] = q4 * values * (1.0 - inject)
        for b in range(2):
            lc_v[b] = jnp.dot(tri_v[0], split_v[b, 0], preferred_element_type=F32)
        for b in range(2):
            k = 2 * pair + b
            for rows, lanes, j in slabs():
                log_cum = lc_v[b, rows, lanes]
                cum = jnp.exp(log_cum)
                inverse = jnp.exp(-log_cum)
                inv_v[k, rows, lanes] = inverse
                pex_v[k, rows, lanes] = jnp.exp(log_cum - ld_v[b, rows, lanes])
                scaled = drive_v[b, rows, lanes] * inverse
                split_store(b, 1, rows.start, lanes, scaled)
                split_store(b, 2, rows.start, lanes, cum * go_v[k, rows, lanes].astype(F32))
                last = rows.start + SLAB
                if last % STEPS == 0:
                    slot = (last // STEPS - 1) * 4 + b * 2 + j
                    sum_s[pair, pl.ds(slot, 1), :] = cum[SLAB - 1 : SLAB]
                    sum_s[pair, pl.ds(8 + slot, 1), :] = scaled[SLAB - 1 : SLAB]
        for b in range(2):
            k = 2 * pair + b
            before_v[k] = jnp.dot(tri_v[1], split_v[b, 1], preferred_element_type=F32)
            tail_v[k] = jnp.dot(tri_v[2], split_v[b, 2], preferred_element_type=F32)
        for b in range(2):
            k = 2 * pair + b
            for s in range(SEQS):
                for j in range(2):
                    slot = s * 4 + b * 2 + j
                    lanes = pl.ds(j * 128, 128)
                    before = before_v[k, pl.ds(s * STEPS + STEPS - 1, 1), lanes]
                    end = sum_s[pair, pl.ds(slot, 1), :]
                    held = sum_s[pair, pl.ds(8 + slot, 1), :]
                    sum_s[pair, pl.ds(8 + slot, 1), :] = end * (before + held)
                    sum_s[pair, pl.ds(16 + slot, 1), :] = tail_v[k, pl.ds(s * STEPS, 1), lanes]
        return carry

    lax.fori_loop(0, PAIRS, local_pair, 0)

    pl.semaphore_wait(barrier, (GROUP - 1) + (NZ - 1) + (NY - 1))

    def remote(src, dst, send, recv, target):
        return pltpu.make_async_remote_copy(
            src_ref=src, dst_ref=dst, send_sem=send, recv_sem=recv,
            device_id=target, device_id_type=pl.DeviceIdType.MESH,
        )

    def in_group(source, landing, send, recv, peer, mine):
        slot = member if mine else peer
        return remote(
            source.at[peer], landing.at[slot], send.at[peer], recv.at[slot], device(y, z, peer)
        )

    def along(axis, landing, send, recv, peer, mine):
        here = z if axis == "z" else y
        target = device(y, peer, member) if axis == "z" else device(peer, z, member)
        slot = here if mine else peer
        return remote(landing.at[here], landing.at[slot], send.at[peer], recv.at[slot], target)

    def group_peers():
        return [lax.rem(member + step, GROUP) for step in range(1, GROUP)]

    def axis_peers(axis):
        here, size = (z, NZ) if axis == "z" else (y, NY)
        return [lax.rem(here + step, size) for step in range(1, size)]

    for peer in group_peers():
        in_group(sum_s, sum_r, g1_send, g1_recv, peer, True).start()
    sum_r[member] = sum_s[member]
    for peer in group_peers():
        in_group(sum_s, sum_r, g1_send, g1_recv, peer, False).wait_recv()

    mult, first, back = pl.ds(0, 8), pl.ds(8, 8), pl.ds(16, 8)

    def total_of(ref, count):
        decay = ref[0, mult]
        state = ref[0, first]
        for j in range(1, count):
            state = ref[j, mult] * state + ref[j, first]
            decay = decay * ref[j, mult]
        adjoint = ref[count - 1, back]
        for j in range(count - 2, -1, -1):
            adjoint = ref[j, mult] * adjoint + ref[j, back]
        return decay, state, adjoint

    def put(ref, index, values):
        for position, value in enumerate(values):
            ref[index, pl.ds(8 * position, 8)] = value

    put(zsum_r, z, total_of(sum_r, GROUP))
    for peer in axis_peers("z"):
        along("z", zsum_r, z1_send, z1_recv, peer, True).start()
    for peer in axis_peers("z"):
        along("z", zsum_r, z1_send, z1_recv, peer, False).wait_recv()
    put(ysum_r, y, total_of(zsum_r, NZ))
    for peer in axis_peers("y"):
        along("y", ysum_r, y1_send, y1_recv, peer, True).start()

    def earlier(ref, count, position, decay, state):
        for j in range(count):
            use = j < position
            state = jnp.where(use, ref[j, mult] * state + ref[j, first], state)
            decay = jnp.where(use, ref[j, mult] * decay, decay)
        return decay, state

    def later(ref, count, position, decay, adjoint):
        for j in range(count - 1, -1, -1):
            use = j > position
            adjoint = jnp.where(use, ref[j, mult] * adjoint + ref[j, back], adjoint)
            decay = jnp.where(use, ref[j, mult] * decay, decay)
        return decay, adjoint

    ones, zeros = jnp.ones((8, 128), F32), jnp.zeros((8, 128), F32)
    z_decay, z_state = earlier(zsum_r, NZ, z, ones, zeros)
    z_fade, z_adjoint = later(zsum_r, NZ, z, ones, zeros)
    for peer in axis_peers("y"):
        along("y", ysum_r, y1_send, y1_recv, peer, False).wait_recv()
    state = z_decay * earlier(ysum_r, NY, y, ones, zeros)[1] + z_state
    adjoint = z_fade * later(ysum_r, NY, y, ones, zeros)[1] + z_adjoint
    for j in range(GROUP):
        ent_s[j, pl.ds(0, 8)] = state
        state = sum_r[j, mult] * state + sum_r[j, first]
    for j in range(GROUP - 1, -1, -1):
        ent_s[j, pl.ds(8, 8)] = adjoint
        adjoint = sum_r[j, mult] * adjoint + sum_r[j, back]
    for peer in group_peers():
        in_group(ent_s, ent_r, g2_send, g2_recv, peer, True).start()
    ent_r[member] = ent_s[member]
    for peer in group_peers():
        in_group(ent_s, ent_r, g2_send, g2_recv, peer, False).wait_recv()

    other = device(y, z, x * NC + (1 - core))

    def core_copy(pair):
        high, low = pair // 4, pl.ds(2 * lax.rem(pair, 4), 2)
        return remote(
            grad_v.at[:, high, low, :, 1 - core], part_v.at[:, high, low],
            core_send.at[pair], core_recv.at[pair], other,
        )

    def out_copy(k):
        lanes = pl.ds(pl.multiple_of(k * BW, BW), BW)
        return pltpu.make_async_copy(out_v.at[k], out_hbm.at[:, lanes], out_sem.at[k])

    def gradient_pair(pair, carry):
        for b in range(2):
            k = 2 * pair + b
            for j in range(2):
                lanes = pl.ds(j * 128, 128)
                sums = [jnp.zeros((8, 128), F32) for _ in range(3)]
                for s in range(SEQS):
                    slot = s * 4 + b * 2 + j
                    entering = ent_r[pair, pl.ds(slot, 1), :]
                    arriving = ent_r[pair, pl.ds(8 + slot, 1), :] * sum_s[pair, pl.ds(slot, 1), :]
                    for top in range(s * STEPS, (s + 1) * STEPS, SLAB):
                        rows = pl.ds(top, SLAB)
                        adj = inv_v[k, rows, lanes] * (tail_v[k, rows, lanes] + arriving)
                        previous = pex_v[k, rows, lanes] * (before_v[k, rows, lanes] + entering)
                        rated = adj * (c_v[k, rows, lanes] - previous * e_v[k, rows, lanes])
                        pre_r = rated * f_v[k, rows, lanes]
                        pre_i = adj * q3_v[k, rows, lanes]
                        dg_v[b, rows, lanes] = adj * q4_v[k, rows, lanes]
                        p_v[b, 0, rows, lanes] = pre_r.astype(BF16)
                        p_v[b, 1, rows, lanes] = pre_i.astype(BF16)
                        for position, value in enumerate((pre_r, pre_i, rated)):
                            for part in range(0, SLAB, 8):
                                sums[position] = sums[position] + value[part : part + 8]
                for position in range(3):
                    vec_s[pair, pl.ds(position * 4 + b * 2 + j, 1), :] = jnp.sum(
                        sums[position], axis=0, keepdims=True
                    )
        for b in range(2):
            k = 2 * pair + b
            across = (((1,), (1,)), ((), ()))
            through = lax.dot_general(p_v[b, 0], w_v[0, k], across, preferred_element_type=F32)
            through += lax.dot_general(p_v[b, 1], w_v[1, k], across, preferred_element_type=F32)
            out_v[k] = (dg_v[b] + through).astype(BF16)
            out_copy(k).start()
        for b in range(2):
            k = 2 * pair + b
            for g in range(2):
                outer = lax.dot_general(
                    x_v[k], p_v[b, g], (((0,), (0,)), ((), ())), preferred_element_type=F32
                )
                grad_v[g, pair // 4, 2 * lax.rem(pair, 4) + b] = outer.reshape(NX, NC, 32, BW)
        core_copy(pair).start()
        return carry

    lax.fori_loop(0, PAIRS, gradient_pair, 0)

    for peer in group_peers():
        in_group(vec_s, vec_r, v1_send, v1_recv, peer, True).start()
    vec_r[member] = vec_s[member]

    def core_sum(pair, carry):
        core_copy(pair).wait_recv()
        high = pair // 4
        for g in range(2):
            for b in range(2):
                at = 2 * lax.rem(pair, 4) + b
                for q in range(NX):
                    part_v[g, high, at, q] = part_v[g, high, at, q] + grad_v[g, high, at, q, core]
        return carry

    lax.fori_loop(0, PAIRS, core_sum, 0)

    here = {"y": y, "z": z, "x": x}

    def index_of(axis, at, whole, halved, side):
        if not whole:
            return (at // 2, lax.rem(at, 2)) if axis == "y" else (at,)
        if axis == "y":
            return (pl.ds(side, 1) if halved else pl.ds(0, 2), pl.ds(0, 2))
        size = SIZES[axis]
        return (pl.ds(side * (size // 2), size // 2) if halved else pl.ds(0, size),)

    def ring(part, number, side):
        (row0, rows), (col0, cols), order = PARTS[part]
        stage, axis, step = rounds_of(order)[number]
        size = SIZES[axis]
        half = size // 2
        toward = 1 if side == 0 else size - 1
        axes = free_axes(order, stage)
        halved = step == 1 and len(axes) > 0
        skipped = step == 1 and not halved and side == 1
        sent = here[axis] + (half - step + 1 if side == 0 else size - half + step - 1)
        came = here[axis] + (half - step if side == 0 else size - half + step)

        def index(target):
            found = []
            for name in "yzx":
                if name == axis:
                    found += index_of(name, lax.rem(target, size), False, False, 0)
                elif name in axes:
                    found += index_of(name, 0, True, halved and name == axes[0], side)
                else:
                    found += index_of(name, here[name], False, False, 0)
            return tuple(found)

        place = dict(here)
        place[axis] = lax.rem(here[axis] + toward, size)
        target = device(place["y"], place["z"], place["x"] * NC + core)
        buffer = ring_bufs[part * ROUNDS + number].at[side]
        payload = (pl.ds(row0, rows), pl.ds(col0, cols))
        copy = remote(
            part_v.at[index(sent) + payload], buffer,
            ring_send.at[part, number, side], ring_recv.at[part, number, side], target,
        )
        return copy, index(came), payload, skipped, axes, halved

    def ring_start(part, number):
        for side in range(2):
            copy, _, _, skipped, _, _ = ring(part, number, side)
            if not skipped:
                copy.start()

    def ring_finish(part, number):
        for side in range(2):
            copy, index, payload, skipped, axes, halved = ring(part, number, side)
            if skipped:
                continue
            copy.wait_recv()
            buffer = ring_bufs[part * ROUNDS + number]
            if len(axes) == 0:
                part_v[index + payload] = part_v[index + payload] + buffer[side]
                continue
            first_axis = axes[0]
            size = SIZES[first_axis] // 2 if halved else SIZES[first_axis]
            position = {"y": 0, "z": 2, "x": 3}[first_axis]
            width = 2 if first_axis == "y" else 1
            base = (size * side) if halved else 0

            def add(i, carry):
                if first_axis == "y":
                    from_, to = (i // 2, lax.rem(i, 2)), ((base + i) // 2, lax.rem(base + i, 2))
                else:
                    from_, to = (i,), (base + i,)
                at = index[:position] + to + index[position + width :] + payload
                part_v[at] = part_v[at] + buffer[(side,) + from_]
                return carry

            lax.fori_loop(0, size, add, 0)

    def ring_wait_sent():
        for part in range(len(PARTS)):
            for number in range(ROUNDS):
                for side in range(2):
                    copy, _, _, skipped, _, _ = ring(part, number, side)
                    if not skipped:
                        copy.wait_send()

    def vector_step(step):
        if step == 0:
            for peer in group_peers():
                in_group(vec_s, vec_r, v1_send, v1_recv, peer, False).wait_recv()
            vecz_r[z] = sum(vec_r[j] for j in range(GROUP))
            for peer in axis_peers("z"):
                along("z", vecz_r, vz_send, vz_recv, peer, True).start()
        elif step == 1:
            for peer in axis_peers("z"):
                along("z", vecz_r, vz_send, vz_recv, peer, False).wait_recv()
            vecy_r[y] = sum(vecz_r[j] for j in range(NZ))
            for peer in axis_peers("y"):
                along("y", vecy_r, vy_send, vy_recv, peer, True).start()
        elif step == 2:
            for peer in axis_peers("y"):
                along("y", vecy_r, vy_send, vy_recv, peer, False).wait_recv()
            veco_r[member] = sum(vecy_r[j] for j in range(NY))
            for peer in group_peers():
                result_copy(peer, True).start()
        else:
            for peer in group_peers():
                result_copy(peer, False).wait_recv()
            for slice_ in range(GROUP):
                for position in range(3):
                    for tile in range(4):
                        lanes = pl.ds(slice_ * 512 + tile * 128, 128)
                        line = veco_r[slice_, pl.ds(position * 4 + tile, 1), :]
                        if position < 2:
                            bg_ref[pl.ds(position, 1), lanes] = line
                        else:
                            rg_ref[:, lanes] = line

    def result_copy(peer, mine):
        slot = member if mine else peer
        return remote(
            veco_r.at[member], veco_r.at[slot], v2_send.at[peer], v2_recv.at[slot],
            device(y, z, peer),
        )

    for part in range(len(PARTS)):
        ring_start(part, 0)
    vector_step(0)
    after = {2: 1, 5: 2, 12: 3}
    for count, (part, number) in enumerate(EVENTS):
        ring_finish(part, number)
        if number + 1 < ROUNDS:
            ring_start(part, number + 1)
        if count in after:
            vector_step(after[count])
    gg_ref[...] = part_v[y // 2, lax.rem(y, 2), z, x]

    for peer in group_peers():
        in_group(sum_s, sum_r, g1_send, g1_recv, peer, True).wait_send()
        in_group(ent_s, ent_r, g2_send, g2_recv, peer, True).wait_send()
        in_group(vec_s, vec_r, v1_send, v1_recv, peer, True).wait_send()
        result_copy(peer, True).wait_send()
    for peer in axis_peers("z"):
        along("z", zsum_r, z1_send, z1_recv, peer, True).wait_send()
        along("z", vecz_r, vz_send, vz_recv, peer, True).wait_send()
    for peer in axis_peers("y"):
        along("y", ysum_r, y1_send, y1_recv, peer, True).wait_send()
        along("y", vecy_r, vy_send, vy_recv, peer, True).wait_send()
    ring_wait_sent()

    def drain(pair, carry):
        core_copy(pair).wait_send()
        out_copy(2 * pair).wait()
        out_copy(2 * pair + 1).wait()
        return carry

    lax.fori_loop(0, PAIRS, drain, 0)


def per_device(inputs, grad_out, gate_weights, gate_biases, decay_rate):
    shape = inputs.shape
    hbm = pl.BlockSpec(memory_space=pl.ANY)
    vmem = pl.BlockSpec(memory_space=pltpu.VMEM)
    dma = pltpu.SemaphoreType.DMA
    block32 = pltpu.VMEM((BLOCKS, ROWS, BW), F32)
    block16 = pltpu.VMEM((BLOCKS, ROWS, BW), BF16)
    scratch = [
        block16, block16, pltpu.VMEM((2, BLOCKS, BW, BW), BF16),
        pltpu.VMEM((2, D), F32), pltpu.VMEM((1, D), F32), block16,
        pltpu.VMEM((3, ROWS, 2 * ROWS), BF16), pltpu.VMEM((2, 2, ROWS, BW), F32),
        pltpu.VMEM((2, ROWS, BW), F32), pltpu.VMEM((2, ROWS, BW), F32),
        pltpu.VMEM((2, ROWS, BW), F32), pltpu.VMEM((2, 3, 2 * ROWS, BW), BF16),
        pltpu.VMEM((2, ROWS, BW), F32), pltpu.VMEM((2, 2, ROWS, BW), BF16),
    ]
    scratch += [block32] * 9
    scratch += [
        pltpu.VMEM((GROUP, 24, 128), F32), pltpu.VMEM((GROUP, 24, 128), F32),
        pltpu.VMEM((NZ, 24, 128), F32), pltpu.VMEM((NY, 24, 128), F32),
        pltpu.VMEM((GROUP, 16, 128), F32), pltpu.VMEM((GROUP, 16, 128), F32),
        pltpu.VMEM((GROUP, 16, 128), F32), pltpu.VMEM((GROUP, 16, 128), F32),
        pltpu.VMEM((NZ, 16, 128), F32), pltpu.VMEM((NY, 16, 128), F32),
        pltpu.VMEM((GROUP, 16, 128), F32),
        pltpu.VMEM((2, 2, NZ, NX, NC, 32, BW), F32), pltpu.VMEM((2, 2, NZ, NX, 32, BW), F32),
        dma((3, BLOCKS)), dma((2,)), dma((BLOCKS,)),
        dma((GROUP,)), dma((GROUP,)), dma((NZ,)), dma((NZ,)),
        dma((NY,)), dma((NY,)), dma((GROUP,)), dma((GROUP,)),
        dma((GROUP,)), dma((GROUP,)), dma((NZ,)), dma((NZ,)),
        dma((NY,)), dma((NY,)), dma((GROUP,)), dma((GROUP,)),
        dma((PAIRS,)), dma((PAIRS,)),
        dma((len(PARTS), ROUNDS, 2)), dma((len(PARTS), ROUNDS, 2)),
    ]
    scratch += [pltpu.VMEM(found, F32) for found in RING_BUFFERS]
    input_grad, gate_grads, bias_grads, rate_grad = pl.pallas_call(
        kernel,
        out_shape=(
            jax.ShapeDtypeStruct((ROWS, D), BF16),
            jax.ShapeDtypeStruct((32, BW), F32),
            jax.ShapeDtypeStruct((2, D), F32),
            jax.ShapeDtypeStruct((1, D), F32),
        ),
        in_specs=[hbm] * 5,
        out_specs=(hbm, vmem, vmem, vmem),
        scratch_shapes=scratch,
        compiler_params=pltpu.CompilerParams(
            collective_id=0, has_side_effects=True, vmem_limit_bytes=60 * 2**20
        ),
    )(
        inputs.reshape(ROWS, D), grad_out.reshape(ROWS, D), gate_weights,
        gate_biases, decay_rate.reshape(1, D),
    )
    return (input_grad.reshape(shape), gate_grads, bias_grads, rate_grad.reshape(D))


def solution(mesh):
    in_specs = (P(None, ("outer", "inner"), None), P(None, ("outer", "inner"), None), P(), P(), P())
    out_specs = (P(None, ("outer", "inner"), None), P(("outer", "inner"), None), P(), P())
    return jax.shard_map(
        per_device, mesh=mesh, in_specs=in_specs, out_specs=out_specs, check_vma=False
    )
```

```python
import functools

import jax
import jax.numpy as jnp
from jax import lax
from jax.experimental import pallas as pl
from jax.experimental.pallas import tpu as pltpu
from jax.sharding import PartitionSpec as P

F32, BF16 = jnp.float32, jnp.bfloat16
rate_gain = 8.0
NY, NZ, NX, NC = 4, 8, 4, 2
GROUP = NX * NC
BLOCKS, BW, D = 16, 256, 4096
SEQS, STEPS = 2, 64
ROWS = SEQS * STEPS
PAIRS = BLOCKS // 2
SLAB = 32
SIZES = {"y": NY, "z": NZ, "x": NX}

HALF = BW // 2

PARTS = (
    ((0, 16, "xyz"), (16, 8, "yxz"), (24, 8, "zxy")),
    ((0, 8, "xyz"), (8, 16, "yxz"), (24, 8, "zxy")),
)


def rounds_of(order):
    rounds = []
    for stage, axis in enumerate(order):
        if stage == 0 or (stage == 1 and order[2] == "z"):
            rounds += [(stage, axis, step) for step in range(1, SIZES[axis] // 2 + 1)]
        else:
            rounds.append((stage, axis, 0))
    return rounds


def free_axes(order, stage):
    return [axis for axis in "yzx" if axis in order[stage + 1 :]]


def lead_shape(axes, halved):
    shape = []
    for position, axis in enumerate(axes):
        half = halved and position == 0
        if axis == "y":
            shape += [1 if half else 2, 2]
        else:
            shape += [SIZES[axis] // 2 if half else SIZES[axis]]
    return tuple(shape)


def landing_buffers():
    places, shapes = {}, []
    for h in range(2):
        for part, (_, rows, order) in enumerate(PARTS[h]):
            for number, (stage, axis, step) in enumerate(rounds_of(order)):
                count = SIZES[axis] if step == 0 else 2
                places[h, part, number] = len(shapes)
                lead = lead_shape(free_axes(order, stage), step == 1)
                shapes.append((count,) + lead + (rows, HALF))
    return places, shapes


LANDING, LANDING_SHAPES = landing_buffers()

EVENTS = [
    (0, 2, 0), (0, 1, 0), (0, 0, 0), (0, 2, 1), "through 0", (0, 1, 1), (1, 2, 0), (0, 2, 2),
    "vector 0", "through 1", (1, 1, 0), (0, 1, 2), (0, 0, 1), (1, 0, 0), (1, 2, 1), (0, 2, 3),
    (0, 1, 3), "vector 1", (0, 0, 2), (1, 2, 2), (0, 2, 4), (1, 0, 1), (0, 1, 4), (1, 1, 1),
    (0, 0, 3), (1, 2, 3), "vector 2", (0, 2, 5), (1, 0, 2), (1, 1, 2), (0, 0, 4), (1, 2, 4),
    (1, 0, 3), (1, 1, 3), "vector 3", (1, 2, 5), (1, 0, 4), (1, 1, 4),
]


def kernel(
    x_hbm, go_hbm, w_hbm, bias_hbm, rate_hbm,
    out_hbm, gg_ref, bg_ref, rg_ref,
    x_v, go_v, w_v, bias_v, rate_v, out_v,
    tri_v, pre_v, ld_v, drive_v, lc_v, split_v, dg_v, p_v,
    inv_v, pex_v, before_v, tail_v, c_v, e_v, f_v, q3_v, q4_v,
    sum_s, sum_r, zsum_r, ysum_r, ent_s, ent_r,
    vec_s, vec_r, vecz_r, vecy_r, veco_r,
    grad_v, part_v,
    in_sem, small_sem, out_sem,
    g1_send, g1_recv, z1_send, z1_recv, y1_send, y1_recv, g2_send, g2_recv,
    v1_send, v1_recv, vz_send, vz_recv, vy_send, vy_recv, v2_send, v2_recv,
    core_send, core_recv, far_send, far_recv,
    *landing,
):
    y = lax.axis_index("outer")
    inner = lax.axis_index("inner")
    z = inner // GROUP
    member = lax.rem(inner, GROUP)
    x = member // NC
    core = lax.rem(member, NC)

    def device(y_at, z_at, member_at):
        return (y_at, z_at * GROUP + member_at)

    barrier = pltpu.get_barrier_semaphore()

    def greet(target):
        pl.semaphore_signal(barrier, inc=1, device_id=target, device_id_type=pl.DeviceIdType.MESH)

    for step in range(1, GROUP):
        greet(device(y, z, lax.rem(member + step, GROUP)))
    for step in range(1, NZ):
        greet(device(y, lax.rem(z + step, NZ), member))
    for step in range(1, NY):
        greet(device(lax.rem(y + step, NY), z, member))

    def start_loads(step, carry):
        blocks = pl.ds(4 * step, 4)
        for b in range(4):
            k = 4 * step + b
            lanes = pl.ds(pl.multiple_of(k * BW, BW), BW)
            pltpu.make_async_copy(x_hbm.at[:, lanes], x_v.at[k], in_sem.at[0, step]).start()
        pltpu.make_async_copy(w_hbm.at[:, blocks], w_v.at[:, blocks], in_sem.at[1, step]).start()
        for b in range(4):
            k = 4 * step + b
            lanes = pl.ds(pl.multiple_of(k * BW, BW), BW)
            pltpu.make_async_copy(go_hbm.at[:, lanes], go_v.at[k], in_sem.at[2, step]).start()
        return carry

    def wait_loads(step):
        blocks = pl.ds(4 * step, 4)
        pltpu.make_async_copy(x_v.at[blocks], x_v.at[blocks], in_sem.at[0, step]).wait()
        pltpu.make_async_copy(w_hbm.at[:, blocks], w_v.at[:, blocks], in_sem.at[1, step]).wait()
        pltpu.make_async_copy(go_v.at[blocks], go_v.at[blocks], in_sem.at[2, step]).wait()

    bias_copy = pltpu.make_async_copy(bias_hbm, bias_v, small_sem.at[0])
    rate_copy = pltpu.make_async_copy(rate_hbm, rate_v, small_sem.at[1])
    bias_copy.start()
    rate_copy.start()
    lax.fori_loop(0, 4, start_loads, 0)

    row = lax.broadcasted_iota(jnp.int32, (ROWS, 2 * ROWS), 0)
    col = lax.broadcasted_iota(jnp.int32, (ROWS, 2 * ROWS), 1)
    col = jnp.where(col >= ROWS, col - ROWS, col)
    same = jnp.where(row >= STEPS, 1, 0) == jnp.where(col >= STEPS, 1, 0)
    tri_v[0] = jnp.where(same & (col <= row), 1.0, 0.0).astype(BF16)
    tri_v[1] = jnp.where(same & (col < row), 1.0, 0.0).astype(BF16)
    tri_v[2] = jnp.where(same & (col >= row), 1.0, 0.0).astype(BF16)

    vec_s[...] = jnp.zeros_like(vec_s)
    sum_s[...] = jnp.zeros_like(sum_s)
    bias_copy.wait()
    rate_copy.wait()

    def slabs():
        for b in range(2):
            for top in range(0, ROWS, SLAB):
                yield b, pl.ds(top, SLAB), pl.ds(b * HALF, HALF)

    def split_store(u, which, top, lanes, value):
        high = value.astype(BF16)
        split_v[u, which, pl.ds(top, SLAB), lanes] = high
        split_v[u, which, pl.ds(ROWS + top, SLAB), lanes] = (value - high.astype(F32)).astype(BF16)

    def gate_columns(k, h):
        lanes = pl.ds(h * HALF, HALF)
        return jnp.concatenate([w_v[0, k, :, lanes], w_v[1, k, :, lanes]], axis=1)

    def local(h, step):
        mine = pl.ds(h * HALF, HALF)
        units = [2 * step, 2 * step + 1]
        if h == 0:
            wait_loads(step)
        for u, m in enumerate(units):
            for b in range(2):
                k = 2 * m + b
                pre_v[u, b] = jnp.dot(x_v[k], gate_columns(k, h), preferred_element_type=F32)
        for u, m in enumerate(units):
            for b, rows, lanes in slabs():
                k = 2 * m + b
                column = pl.ds(pl.multiple_of(k * BW + h * HALF, HALF), HALF)
                rate = rate_v[0:1, column]
                pre_r = pre_v[u, b, rows, pl.ds(0, HALF)] + bias_v[0:1, column]
                pre_i = pre_v[u, b, rows, pl.ds(HALF, HALF)] + bias_v[1:2, column]
                recur = 1.0 / (1.0 + jnp.exp(-pre_r))
                inject = 1.0 / (1.0 + jnp.exp(-pre_i))
                values = x_v[k, rows, mine].astype(F32)
                log_decay = (-rate_gain * rate) * recur
                decay = jnp.exp(log_decay)
                series = -log_decay * (
                    1.0 + log_decay * (0.5 + log_decay * (1.0 / 6.0 + log_decay * (1.0 / 24.0)))
                )
                lost = jnp.where(log_decay > -0.1, series, 1.0 - decay)
                square = lost * (1.0 + decay)
                inverse_scale = lax.rsqrt(square)
                scale = square * inverse_scale
                driven = inject * values
                drive_v[u, rows, lanes] = scale * driven
                ld_v[u, rows, lanes] = log_decay
                split_store(u, 0, rows.start, lanes, log_decay)
                gained = rate_gain * recur
                e = gained * decay
                e_v[h, m, rows, lanes] = e
                c_v[h, m, rows, lanes] = e * decay * driven * inverse_scale
                f_v[h, m, rows, lanes] = rate * (1.0 - recur)
                q4 = scale * inject
                q4_v[h, m, rows, lanes] = q4
                q3_v[h, m, rows, lanes] = q4 * values * (1.0 - inject)
        for u, m in enumerate(units):
            lc_v[u] = jnp.dot(tri_v[0], split_v[u, 0], preferred_element_type=F32)
        for u, m in enumerate(units):
            for b, rows, lanes in slabs():
                log_cum = lc_v[u, rows, lanes]
                cum = jnp.exp(log_cum)
                inverse = jnp.exp(-log_cum)
                inv_v[h, m, rows, lanes] = inverse
                pex_v[h, m, rows, lanes] = jnp.exp(log_cum - ld_v[u, rows, lanes])
                scaled = drive_v[u, rows, lanes] * inverse
                split_store(u, 1, rows.start, lanes, scaled)
                upstream = go_v[2 * m + b, rows, mine].astype(F32)
                split_store(u, 2, rows.start, lanes, cum * upstream)
                last = rows.start + SLAB
                if last % STEPS == 0:
                    slot = (last // STEPS - 1) * 2 + b
                    sum_s[h, m, pl.ds(slot, 1), :] = cum[SLAB - 1 : SLAB]
                    sum_s[h, m, pl.ds(4 + slot, 1), :] = scaled[SLAB - 1 : SLAB]
        for u, m in enumerate(units):
            before_v[h, m] = jnp.dot(tri_v[1], split_v[u, 1], preferred_element_type=F32)
            tail_v[h, m] = jnp.dot(tri_v[2], split_v[u, 2], preferred_element_type=F32)
        for u, m in enumerate(units):
            for s in range(SEQS):
                for b in range(2):
                    slot = s * 2 + b
                    lanes = pl.ds(b * HALF, HALF)
                    before = before_v[h, m, pl.ds(s * STEPS + STEPS - 1, 1), lanes]
                    end = sum_s[h, m, pl.ds(slot, 1), :]
                    held = sum_s[h, m, pl.ds(4 + slot, 1), :]
                    sum_s[h, m, pl.ds(4 + slot, 1), :] = end * (before + held)
                    sum_s[h, m, pl.ds(8 + slot, 1), :] = tail_v[h, m, pl.ds(s * STEPS, 1), lanes]

    def local_steps(h, start, stop):
        def body(step, carry):
            local(h, step)
            return carry

        lax.fori_loop(start, stop, body, 0)

    def remote(src, dst, send, recv, target):
        return pltpu.make_async_remote_copy(
            src_ref=src, dst_ref=dst, send_sem=send, recv_sem=recv,
            device_id=target, device_id_type=pl.DeviceIdType.MESH,
        )

    def in_group(source, landing, send, recv, peer):
        return remote(source.at[peer], landing.at[member], send, recv, device(y, z, peer))

    def along(axis, landing, send, recv, peer):
        here = z if axis == "z" else y
        target = device(y, peer, member) if axis == "z" else device(peer, z, member)
        return remote(landing.at[here], landing.at[here], send, recv, target)

    def all_of(landing, send, recv, count):
        every = landing.at[pl.ds(0, count - 1)]
        return remote(every, every, send, recv, device(y, z, x * NC + (1 - core)))

    def group_all(source, landing, send, recv):
        return all_of(landing, send, recv, GROUP)

    def along_all(axis, landing, send, recv):
        return all_of(landing, send, recv, SIZES[axis])

    def group_peers():
        return [lax.rem(member + step, GROUP) for step in range(1, GROUP)]

    def axis_peers(axis):
        here, size = (z, NZ) if axis == "z" else (y, NY)
        return [lax.rem(here + step, size) for step in range(1, size)]

    mult, first, back = pl.ds(0, 4), pl.ds(4, 4), pl.ds(8, 4)
    ones, zeros = jnp.ones((4, 128), F32), jnp.zeros((4, 128), F32)

    def total_of(ref, count):
        decay = ref[0, mult]
        state = ref[0, first]
        for j in range(1, count):
            state = ref[j, mult] * state + ref[j, first]
            decay = decay * ref[j, mult]
        adjoint = ref[count - 1, back]
        for j in range(count - 2, -1, -1):
            adjoint = ref[j, mult] * adjoint + ref[j, back]
        return decay, state, adjoint

    def put(ref, index, values):
        for position, value in enumerate(values):
            ref[index, pl.ds(4 * position, 4)] = value
        ref[index, pl.ds(12, 4)] = zeros

    def earlier(ref, count, position, decay, state):
        for j in range(count):
            use = j < position
            state = jnp.where(use, ref[j, mult] * state + ref[j, first], state)
            decay = jnp.where(use, ref[j, mult] * decay, decay)
        return decay, state

    def later(ref, count, position, decay, adjoint):
        for j in range(count - 1, -1, -1):
            use = j > position
            adjoint = jnp.where(use, ref[j, mult] * adjoint + ref[j, back], adjoint)
            decay = jnp.where(use, ref[j, mult] * decay, decay)
        return decay, adjoint

    def group_1(h):
        return sum_s.at[h], sum_r.at[h], g1_send.at[h], g1_recv.at[h]

    def group_2(h):
        return ent_s.at[h], ent_r.at[h], g2_send.at[h], g2_recv.at[h]

    def along_z(h):
        return "z", zsum_r.at[h], z1_send.at[h], z1_recv.at[h]

    def along_y(h):
        return "y", ysum_r.at[h], y1_send.at[h], y1_recv.at[h]

    def summaries_out(h):
        for peer in group_peers():
            in_group(*group_1(h), peer).start()
        sum_r[h, member] = sum_s[h, member]

    def to_z(h):
        group_all(*group_1(h)).wait_recv()
        put(zsum_r.at[h], z, total_of(sum_r.at[h], GROUP))
        for peer in axis_peers("z"):
            along(*along_z(h), peer).start()

    def to_y(h):
        along_all(*along_z(h)).wait_recv()
        put(ysum_r.at[h], y, total_of(zsum_r.at[h], NZ))
        for peer in axis_peers("y"):
            along(*along_y(h), peer).start()

    def to_members(h):
        z_decay, z_state = earlier(zsum_r.at[h], NZ, z, ones, zeros)
        z_fade, z_adjoint = later(zsum_r.at[h], NZ, z, ones, zeros)
        along_all(*along_y(h)).wait_recv()
        state = z_decay * earlier(ysum_r.at[h], NY, y, ones, zeros)[1] + z_state
        adjoint = z_fade * later(ysum_r.at[h], NY, y, ones, zeros)[1] + z_adjoint
        for j in range(GROUP):
            ent_s[h, j, pl.ds(0, 4)] = state
            state = sum_r[h, j, mult] * state + sum_r[h, j, first]
        for j in range(GROUP - 1, -1, -1):
            ent_s[h, j, pl.ds(4, 4)] = adjoint
            adjoint = sum_r[h, j, mult] * adjoint + sum_r[h, j, back]
        for peer in group_peers():
            in_group(*group_2(h), peer).start()
        ent_r[h, member] = ent_s[h, member]

    def entered(h):
        group_all(*group_2(h)).wait_recv()

    def summaries_sent():
        for h in range(2):
            group_all(*group_1(h)).wait_send()
            group_all(*group_2(h)).wait_send()
            along_all(*along_z(h)).wait_send()
            along_all(*along_y(h)).wait_send()

    other = device(y, z, x * NC + (1 - core))

    def core_copy(h, m):
        high, low = m // 4, pl.ds(2 * lax.rem(m, 4), 2)
        return remote(
            grad_v.at[h, :, high, low, :, 1 - core], part_v.at[h, :, high, low],
            core_send.at[h], core_recv.at[h], other,
        )

    def core_all(h):
        return remote(part_v.at[h], part_v.at[h], core_send.at[h], core_recv.at[h], other)

    def gradient(h, step):
        units = [2 * step, 2 * step + 1]
        for m in units:
            for b in range(2):
                k = 2 * m + b
                lanes = pl.ds(b * HALF, HALF)
                sums = [jnp.zeros((8, 128), F32) for _ in range(3)]
                for s in range(SEQS):
                    slot = s * 2 + b
                    entering = ent_r[h, m, pl.ds(slot, 1), :]
                    arriving = ent_r[h, m, pl.ds(4 + slot, 1), :] * sum_s[h, m, pl.ds(slot, 1), :]
                    for top in range(s * STEPS, (s + 1) * STEPS, SLAB):
                        rows = pl.ds(top, SLAB)
                        at = (h, m, rows, lanes)
                        adj = inv_v[at] * (tail_v[at] + arriving)
                        previous = pex_v[at] * (before_v[at] + entering)
                        rated = adj * (c_v[at] - previous * e_v[at])
                        pre_r = rated * f_v[at]
                        pre_i = adj * q3_v[at]
                        dg_v[at] = adj * q4_v[at]
                        p_v[k, h, rows, pl.ds(0, HALF)] = pre_r.astype(BF16)
                        p_v[k, h, rows, pl.ds(HALF, HALF)] = pre_i.astype(BF16)
                        for position, value in enumerate((pre_r, pre_i, rated)):
                            for part in range(0, SLAB, 8):
                                sums[position] = sums[position] + value[part : part + 8]
                for position in range(3):
                    line = position * 4 + h * 2 + b
                    vec_s[m, pl.ds(line, 1), :] = jnp.sum(sums[position], axis=0, keepdims=True)
        for m in units:
            for b in range(2):
                k = 2 * m + b
                outer = lax.dot_general(
                    x_v[k], p_v[k, h], (((0,), (0,)), ((), ())), preferred_element_type=F32
                )
                for g in range(2):
                    grad_v[h, g, m // 4, 2 * lax.rem(m, 4) + b] = outer[
                        :, g * HALF : (g + 1) * HALF
                    ].reshape(NX, NC, 32, HALF)
            core_copy(h, m).start()

    def gradient_steps(h, start, stop):
        def body(step, carry):
            gradient(h, step)
            return carry

        lax.fori_loop(start, stop, body, 0)

    def out_copy(k):
        lanes = pl.ds(pl.multiple_of(k * BW, BW), BW)
        return pltpu.make_async_copy(out_v.at[k], out_hbm.at[:, lanes], out_sem)

    def through(half):
        def body(m, carry):
            for b in range(2):
                k = 2 * m + b
                across = (((1,), (1,)), ((), ()))
                for h in range(2):
                    back_in = lax.dot_general(
                        p_v[k, h], gate_columns(k, h), across, preferred_element_type=F32
                    )
                    total = back_in if h == 0 else total + back_in
                for h in range(2):
                    mine = pl.ds(h * HALF, HALF)
                    direct = dg_v[h, m, :, pl.ds(b * HALF, HALF)]
                    out_v[k, :, mine] = (direct + total[:, h * HALF : (h + 1) * HALF]).astype(BF16)
                out_copy(k).start()
            return carry

        lax.fori_loop(half * 4, half * 4 + 4, body, 0)

    def core_sum(h):
        core_all(h).wait_recv()

        def body(m, carry):
            high = m // 4
            for g in range(2):
                for b in range(2):
                    at = 2 * lax.rem(m, 4) + b
                    part_v[h, g, high, at] = part_v[h, g, high, at] + grad_v[h, g, high, at, :, core]
            return carry

        lax.fori_loop(0, PAIRS, body, 0)

    here = {"y": y, "z": z, "x": x}

    def index_of(axis, at, whole, halved, side):
        if not whole:
            return (at // 2, lax.rem(at, 2)) if axis == "y" else (at,)
        if axis == "y":
            return (pl.ds(side, 1) if halved else pl.ds(0, 2), pl.ds(0, 2))
        size = SIZES[axis]
        return (pl.ds(side * (size // 2), size // 2) if halved else pl.ds(0, size),)

    def view(h, part, stage, target, halved, side):
        row0, rows, order = PARTS[h][part]
        axis, axes = order[stage], free_axes(order, stage)
        found = (h,)
        for name in "yzx":
            if name == axis:
                found += index_of(name, target, False, False, 0)
            elif name in axes:
                found += index_of(name, 0, True, halved and name == axes[0], side)
            else:
                found += index_of(name, here[name], False, False, 0)
        return found + (pl.ds(row0, rows), slice(None))

    def far_all(h, part, number):
        buffer = landing[LANDING[h, part, number]]
        axis, step = rounds_of(PARTS[h][part][2])[number][1:]
        every = buffer if step > 0 else buffer.at[pl.ds(0, SIZES[axis] - 1)]
        at = LANDING[h, part, number]
        return remote(every, every, far_send.at[at], far_recv.at[at], other)

    def ring_copy(h, part, number, side):
        stage, axis, step = rounds_of(PARTS[h][part][2])[number]
        size = SIZES[axis]
        half = size // 2
        sent = here[axis] + (half - step + 1 if side == 0 else size - half + step - 1)
        place = dict(here)
        place[axis] = lax.rem(here[axis] + (1 if side == 0 else size - 1), size)
        at = LANDING[h, part, number]
        return remote(
            part_v.at[view(h, part, stage, lax.rem(sent, size), step == 1, side)],
            landing[LANDING[h, part, number]].at[side], far_send.at[at], far_recv.at[at],
            device(place["y"], place["z"], place["x"] * NC + core),
        )

    def direct_copy(h, part, number, peer):
        stage, axis, _ = rounds_of(PARTS[h][part][2])[number]
        place = dict(here)
        place[axis] = peer
        at = LANDING[h, part, number]
        return remote(
            part_v.at[view(h, part, stage, peer, False, 0)],
            landing[LANDING[h, part, number]].at[here[axis]], far_send.at[at], far_recv.at[at],
            device(place["y"], place["z"], place["x"] * NC + core),
        )

    def copies_out(h, part, number):
        _, axis, step = rounds_of(PARTS[h][part][2])[number]
        if step > 0:
            return [ring_copy(h, part, number, side) for side in range(2)]
        peers = [lax.rem(here[axis] + far, SIZES[axis]) for far in range(1, SIZES[axis])]
        return [direct_copy(h, part, number, peer) for peer in peers]

    def far_start(h, part, number):
        for copy in copies_out(h, part, number):
            copy.start()

    def add_landed(at, axes, halved, side, buffer, slots):
        if len(axes) == 0:
            part_v[at] = part_v[at] + sum(buffer[slot] for slot in slots)
            return
        axis = axes[0]
        size = SIZES[axis] // 2 if halved else SIZES[axis]
        position = 1 + {"y": 0, "z": 2, "x": 3}[axis]
        width = 2 if axis == "y" else 1
        base = size * side if halved else 0

        def body(i, carry):
            if axis == "y":
                from_, to = (i // 2, lax.rem(i, 2)), ((base + i) // 2, lax.rem(base + i, 2))
            else:
                from_, to = (i,), (base + i,)
            place = at[:position] + to + at[position + width :]
            part_v[place] = part_v[place] + sum(buffer[(slot,) + from_] for slot in slots)
            return carry

        lax.fori_loop(0, size, body, 0)

    def far_finish(h, part, number):
        order = PARTS[h][part][2]
        stage, axis, step = rounds_of(order)[number]
        size, axes = SIZES[axis], free_axes(order, stage)
        buffer = landing[LANDING[h, part, number]]
        far_all(h, part, number).wait_recv()
        if step == 0:
            peers = [lax.rem(here[axis] + far, size) for far in range(1, size)]
            at = view(h, part, stage, here[axis], False, 0)
            add_landed(at, axes, False, 0, buffer, peers)
            return
        half = size // 2
        for side in range(2):
            came = here[axis] + (half - step if side == 0 else size - half + step)
            at = view(h, part, stage, lax.rem(came, size), step == 1, side)
            add_landed(at, axes, step == 1, side, buffer, [side])

    vector_1 = (vec_s, vec_r, v1_send, v1_recv)
    vector_z = ("z", vecz_r, vz_send, vz_recv)
    vector_y = ("y", vecy_r, vy_send, vy_recv)

    vector_2 = (veco_r, veco_r, v2_send, v2_recv)

    def vector_copy(peer):
        return remote(veco_r.at[member], veco_r.at[member], v2_send, v2_recv, device(y, z, peer))

    def vector_out():
        for peer in group_peers():
            in_group(*vector_1, peer).start()
        vec_r[member] = vec_s[member]

    def vector_step(step):
        if step == 0:
            group_all(*vector_1).wait_recv()
            vecz_r[z] = sum(vec_r[j] for j in range(GROUP))
            for peer in axis_peers("z"):
                along(*vector_z, peer).start()
        elif step == 1:
            along_all(*vector_z).wait_recv()
            vecy_r[y] = sum(vecz_r[j] for j in range(NZ))
            for peer in axis_peers("y"):
                along(*vector_y, peer).start()
        elif step == 2:
            along_all(*vector_y).wait_recv()
            veco_r[member] = sum(vecy_r[j] for j in range(NY))
            for peer in group_peers():
                vector_copy(peer).start()
        else:
            group_all(*vector_2).wait_recv()
            for j in range(GROUP):
                for position in range(3):
                    for h in range(2):
                        for b in range(2):
                            lanes = pl.ds((2 * j + b) * BW + h * HALF, HALF)
                            line = veco_r[j, pl.ds(position * 4 + h * 2 + b, 1), :]
                            if position < 2:
                                bg_ref[pl.ds(position, 1), lanes] = line
                            else:
                                rg_ref[:, lanes] = line

    local_steps(0, 0, 4)
    pl.semaphore_wait(barrier, (GROUP - 1) + (NZ - 1) + (NY - 1))
    summaries_out(0)
    local_steps(1, 0, 3)
    to_z(0)
    local_steps(1, 3, 4)
    summaries_out(1)
    to_y(0)
    to_z(1)
    to_members(0)
    to_y(1)
    entered(0)
    gradient_steps(0, 0, 2)
    to_members(1)
    gradient_steps(0, 2, 4)
    core_sum(0)
    for part in range(3):
        far_start(0, part, 0)
    entered(1)
    gradient_steps(1, 0, 4)
    vector_out()
    core_sum(1)
    for part in range(3):
        far_start(1, part, 0)
    for event in EVENTS:
        if isinstance(event, str):
            kind, number = event.split()
            (through if kind == "through" else vector_step)(int(number))
            continue
        h, part, number = event
        far_finish(h, part, number)
        if number + 1 < len(rounds_of(PARTS[h][part][2])):
            far_start(h, part, number + 1)
    for h in range(2):
        gg_ref[:, pl.ds(h * HALF, HALF)] = part_v[h, y // 2, lax.rem(y, 2), z, x]

    summaries_sent()
    group_all(*vector_1).wait_send()
    group_all(*vector_2).wait_send()
    along_all(*vector_z).wait_send()
    along_all(*vector_y).wait_send()
    for h, part, number in LANDING:
        far_all(h, part, number).wait_send()
    for h in range(2):
        core_all(h).wait_send()
    pltpu.make_async_copy(out_v, out_v, out_sem).wait()


def finish(*refs):
    sources, results, held, sem = refs[:4], refs[4:8], refs[8:12], refs[12]
    count = 0
    pairs = []
    for source, result, hold in zip(sources, results, held):
        rows = source.shape[0]
        size = 16 if rows == ROWS else rows
        for top in range(0, rows, size):
            at = pl.ds(top, size)
            pairs.append((
                pltpu.make_async_copy(source.at[at], hold.at[at], sem.at[0, count]),
                pltpu.make_async_copy(hold.at[at], result.at[at], sem.at[1, count]),
            ))
            count += 1
    for into, _ in pairs:
        into.start()
    for into, out in pairs:
        into.wait()
        out.start()
    for _, out in pairs:
        out.wait()


def per_device(inputs, grad_out, gate_weights, gate_biases, decay_rate):
    shape = inputs.shape
    hbm = pl.BlockSpec(memory_space=pl.ANY)
    vmem = pl.BlockSpec(memory_space=pltpu.VMEM)
    dma = pltpu.SemaphoreType.DMA
    block32 = pltpu.VMEM((2, PAIRS, ROWS, BW), F32)
    block16 = pltpu.VMEM((BLOCKS, ROWS, BW), BF16)
    unit32 = pltpu.VMEM((2, ROWS, BW), F32)
    scratch = [
        block16, block16, pltpu.VMEM((2, BLOCKS, BW, BW), BF16),
        pltpu.VMEM((2, D), F32), pltpu.VMEM((1, D), F32), block16,
        pltpu.VMEM((3, ROWS, 2 * ROWS), BF16), pltpu.VMEM((2, 2, ROWS, BW), F32),
        unit32, unit32, unit32, pltpu.VMEM((2, 3, 2 * ROWS, BW), BF16),
        block32, pltpu.VMEM((BLOCKS, 2, ROWS, BW), BF16),
    ]
    scratch += [block32] * 9
    scratch += [
        pltpu.VMEM((2, GROUP, 16, 128), F32), pltpu.VMEM((2, GROUP, 16, 128), F32),
        pltpu.VMEM((2, NZ, 16, 128), F32), pltpu.VMEM((2, NY, 16, 128), F32),
        pltpu.VMEM((2, GROUP, 8, 128), F32), pltpu.VMEM((2, GROUP, 8, 128), F32),
        pltpu.VMEM((GROUP, 16, 128), F32), pltpu.VMEM((GROUP, 16, 128), F32),
        pltpu.VMEM((NZ, 16, 128), F32), pltpu.VMEM((NY, 16, 128), F32),
        pltpu.VMEM((GROUP, 16, 128), F32),
        pltpu.VMEM((2, 2, 2, NZ, NX, NC, 32, HALF), F32),
        pltpu.VMEM((2, 2, 2, NZ, NX, 32, HALF), F32),
        dma((3, 4)), dma((2,)), dma(()),
        dma((2,)), dma((2,)), dma((2,)), dma((2,)), dma((2,)), dma((2,)), dma((2,)), dma((2,)),
        dma(()), dma(()), dma(()), dma(()), dma(()), dma(()), dma(()), dma(()),
        dma((2,)), dma((2,)), dma((len(LANDING),)), dma((len(LANDING),)),
    ]
    scratch += [pltpu.VMEM(found, F32) for found in LANDING_SHAPES]
    shapes = (
        jax.ShapeDtypeStruct((ROWS, D), BF16),
        jax.ShapeDtypeStruct((32, BW), F32),
        jax.ShapeDtypeStruct((2, D), F32),
        jax.ShapeDtypeStruct((1, D), F32),
    )
    results = pl.pallas_call(
        kernel,
        out_shape=shapes,
        in_specs=[hbm] * 5,
        out_specs=(hbm, vmem, vmem, vmem),
        scratch_shapes=scratch,
        compiler_params=pltpu.CompilerParams(
            collective_id=0, has_side_effects=True, vmem_limit_bytes=60 * 2**20
        ),
    )(
        inputs.reshape(ROWS, D), grad_out.reshape(ROWS, D), gate_weights,
        gate_biases, decay_rate.reshape(1, D),
    )
    input_grad, gate_grads, bias_grads, rate_grad = pl.pallas_call(
        finish, out_shape=shapes, in_specs=[hbm] * 4, out_specs=[hbm] * 4,
        scratch_shapes=[pltpu.VMEM(found.shape, found.dtype) for found in shapes] + [dma((2, 11))],
    )(*results)
    return (input_grad.reshape(shape), gate_grads, bias_grads, rate_grad.reshape(D))


def solution(mesh):
    in_specs = (P(None, ("outer", "inner"), None), P(None, ("outer", "inner"), None), P(), P(), P())
    out_specs = (P(None, ("outer", "inner"), None), P(("outer", "inner"), None), P(), P())
    return jax.shard_map(
        per_device, mesh=mesh, in_specs=in_specs, out_specs=out_specs, check_vma=False
    )
```

```python
import functools

import jax
import jax.numpy as jnp
from jax import lax
from jax.experimental import pallas as pl
from jax.experimental.pallas import tpu as pltpu
from jax.sharding import PartitionSpec as P

F32, BF16 = jnp.float32, jnp.bfloat16
rate_gain = 8.0
NY, NZ, NX, NC = 4, 8, 4, 2
GROUP = NX * NC
BLOCKS, BW, D = 16, 256, 4096
SEQS, STEPS = 2, 64
ROWS = SEQS * STEPS
PAIRS = BLOCKS // 2
SLAB = 32
SIZES = {"y": NY, "z": NZ, "x": NX}

HALF = BW // 2

PARTS = (
    ((0, 8, "zyx"), (8, 16, "zxy"), (24, 8, "xyz")),
    ((0, 16, "yxz"), (16, 8, "xyz"), (24, 8, "xyz")),
)


def rounds_of(order):
    rounds = []
    for stage, axis in enumerate(order):
        if stage == 0:
            rounds += [(stage, axis, step) for step in range(1, SIZES[axis] // 2 + 1)]
        else:
            rounds.append((stage, axis, 0))
    return rounds


def free_axes(order, stage):
    return [axis for axis in "yzx" if axis in order[stage + 1 :]]


def lead_shape(axes, halved):
    shape = []
    for position, axis in enumerate(axes):
        half = halved and position == 0
        if axis == "y":
            shape += [1 if half else 2, 2]
        else:
            shape += [SIZES[axis] // 2 if half else SIZES[axis]]
    return tuple(shape)


def landing_buffers():
    places, shapes = {}, []
    for h in range(2):
        for part, (_, rows, order) in enumerate(PARTS[h]):
            for number, (stage, axis, step) in enumerate(rounds_of(order)):
                count = SIZES[axis] if step == 0 else 2
                places[h, part, number] = len(shapes)
                lead = lead_shape(free_axes(order, stage), step == 1)
                shapes.append((count,) + lead + (rows, HALF))
    return places, shapes


LANDING, LANDING_SHAPES = landing_buffers()

EVENTS = [
    (0, 0, 0), (0, 2, 0), (0, 1, 0), (0, 0, 1), "through 0", (0, 2, 1), (0, 1, 1), "through 1",
    (1, 1, 0), (0, 0, 2), "vector 0", (1, 0, 0), (1, 2, 0), "through 2", (0, 2, 2), (0, 1, 2),
    (0, 0, 3), (1, 1, 1), "vector 1", "through 3", (1, 2, 1), (0, 2, 3), (1, 0, 1), (0, 1, 3),
    "vector 2", (0, 0, 4), (1, 1, 2), (1, 2, 2), (1, 0, 2), "vector 3", (0, 1, 4), (0, 0, 5),
    (1, 1, 3), (1, 2, 3), (0, 1, 5), (1, 0, 3),
]


def kernel(
    x_hbm, go_hbm, w_hbm, bias_hbm, rate_hbm,
    out_hbm, gg_ref, bg_ref, rg_ref,
    x_v, go_v, w_v, bias_v, rate_v, out_v,
    tri_v, pre_v, ld_v, drive_v, lc_v, split_v, dg_v, p_v,
    inv_v, pex_v, before_v, tail_v, c_v, e_v, f_v, q3_v, q4_v,
    sum_s, sum_r, zsum_r, ysum_r, ent_s, ent_r,
    vec_s, vec_r, vecz_r, vecy_r, veco_r,
    grad_v, part_v,
    in_sem, small_sem, out_sem,
    g1_send, g1_recv, z1_send, z1_recv, y1_send, y1_recv, g2_send, g2_recv,
    v1_send, v1_recv, vz_send, vz_recv, vy_send, vy_recv, v2_send, v2_recv,
    core_send, core_recv, far_send, far_recv,
    *landing,
):
    y = lax.axis_index("outer")
    inner = lax.axis_index("inner")
    z = inner // GROUP
    member = lax.rem(inner, GROUP)
    x = member // NC
    core = lax.rem(member, NC)

    def device(y_at, z_at, member_at):
        return (y_at, z_at * GROUP + member_at)

    barrier = pltpu.get_barrier_semaphore()

    def greet(target):
        pl.semaphore_signal(barrier, inc=1, device_id=target, device_id_type=pl.DeviceIdType.MESH)

    for step in range(1, GROUP):
        greet(device(y, z, lax.rem(member + step, GROUP)))
    for step in range(1, NZ):
        greet(device(y, lax.rem(z + step, NZ), member))
    for step in range(1, NY):
        greet(device(lax.rem(y + step, NY), z, member))

    def chip_at(turn):
        return lax.rem(x + 1 + turn, NX)

    def start_loads(turn, carry):
        step = chip_at(turn)
        blocks = pl.ds(4 * step, 4)
        for b in range(4):
            k = 4 * step + b
            lanes = pl.ds(pl.multiple_of(k * BW, BW), BW)
            pltpu.make_async_copy(x_hbm.at[:, lanes], x_v.at[k], in_sem.at[0, step]).start()
        pltpu.make_async_copy(w_hbm.at[:, blocks], w_v.at[:, blocks], in_sem.at[1, step]).start()
        for b in range(4):
            k = 4 * step + b
            lanes = pl.ds(pl.multiple_of(k * BW, BW), BW)
            pltpu.make_async_copy(go_hbm.at[:, lanes], go_v.at[k], in_sem.at[2, step]).start()
        return carry

    def wait_loads(step):
        blocks = pl.ds(4 * step, 4)
        pltpu.make_async_copy(x_v.at[blocks], x_v.at[blocks], in_sem.at[0, step]).wait()
        pltpu.make_async_copy(w_hbm.at[:, blocks], w_v.at[:, blocks], in_sem.at[1, step]).wait()
        pltpu.make_async_copy(go_v.at[blocks], go_v.at[blocks], in_sem.at[2, step]).wait()

    bias_copy = pltpu.make_async_copy(bias_hbm, bias_v, small_sem.at[0])
    rate_copy = pltpu.make_async_copy(rate_hbm, rate_v, small_sem.at[1])
    bias_copy.start()
    rate_copy.start()
    lax.fori_loop(0, 4, start_loads, 0)

    row = lax.broadcasted_iota(jnp.int32, (ROWS, 2 * ROWS), 0)
    col = lax.broadcasted_iota(jnp.int32, (ROWS, 2 * ROWS), 1)
    col = jnp.where(col >= ROWS, col - ROWS, col)
    same = jnp.where(row >= STEPS, 1, 0) == jnp.where(col >= STEPS, 1, 0)
    tri_v[0] = jnp.where(same & (col <= row), 1.0, 0.0).astype(BF16)
    tri_v[1] = jnp.where(same & (col < row), 1.0, 0.0).astype(BF16)
    tri_v[2] = jnp.where(same & (col >= row), 1.0, 0.0).astype(BF16)

    vec_s[...] = jnp.zeros_like(vec_s)
    sum_s[...] = jnp.zeros_like(sum_s)
    bias_copy.wait()
    rate_copy.wait()

    def slabs():
        for b in range(2):
            for top in range(0, ROWS, SLAB):
                yield b, pl.ds(top, SLAB), pl.ds(b * HALF, HALF)

    def split_store(u, which, top, lanes, value):
        high = value.astype(BF16)
        split_v[u, which, pl.ds(top, SLAB), lanes] = high
        split_v[u, which, pl.ds(ROWS + top, SLAB), lanes] = (value - high.astype(F32)).astype(BF16)

    def gate_columns(k, h):
        lanes = pl.ds(h * HALF, HALF)
        return jnp.concatenate([w_v[0, k, :, lanes], w_v[1, k, :, lanes]], axis=1)

    def local(h, step):
        mine = pl.ds(h * HALF, HALF)
        units = [2 * step, 2 * step + 1]
        if h == 0:
            wait_loads(step)
        for u, m in enumerate(units):
            for b in range(2):
                k = 2 * m + b
                pre_v[u, b] = jnp.dot(x_v[k], gate_columns(k, h), preferred_element_type=F32)
        for u, m in enumerate(units):
            for b, rows, lanes in slabs():
                k = 2 * m + b
                column = pl.ds(pl.multiple_of(k * BW + h * HALF, HALF), HALF)
                rate = rate_v[0:1, column]
                pre_r = pre_v[u, b, rows, pl.ds(0, HALF)] + bias_v[0:1, column]
                pre_i = pre_v[u, b, rows, pl.ds(HALF, HALF)] + bias_v[1:2, column]
                recur = 1.0 / (1.0 + jnp.exp(-pre_r))
                inject = 1.0 / (1.0 + jnp.exp(-pre_i))
                values = x_v[k, rows, mine].astype(F32)
                log_decay = (-rate_gain * rate) * recur
                decay = jnp.exp(log_decay)
                series = -log_decay * (
                    1.0 + log_decay * (0.5 + log_decay * (1.0 / 6.0 + log_decay * (1.0 / 24.0)))
                )
                lost = jnp.where(log_decay > -0.1, series, 1.0 - decay)
                square = lost * (1.0 + decay)
                inverse_scale = lax.rsqrt(square)
                scale = square * inverse_scale
                driven = inject * values
                drive_v[u, rows, lanes] = scale * driven
                ld_v[u, rows, lanes] = log_decay
                split_store(u, 0, rows.start, lanes, log_decay)
                at = (h, m, rows, lanes)
                e_v[at], c_v[at], f_v[at] = decay, inverse_scale, recur
                q4_v[at], q3_v[at] = scale, inject
        for u, m in enumerate(units):
            lc_v[u] = jnp.dot(tri_v[0], split_v[u, 0], preferred_element_type=F32)
        for u, m in enumerate(units):
            for b, rows, lanes in slabs():
                log_cum = lc_v[u, rows, lanes]
                cum = jnp.exp(log_cum)
                inverse = jnp.exp(-log_cum)
                inv_v[h, m, rows, lanes] = inverse
                pex_v[h, m, rows, lanes] = jnp.exp(log_cum - ld_v[u, rows, lanes])
                scaled = drive_v[u, rows, lanes] * inverse
                split_store(u, 1, rows.start, lanes, scaled)
                upstream = go_v[2 * m + b, rows, mine].astype(F32)
                split_store(u, 2, rows.start, lanes, cum * upstream)
                last = rows.start + SLAB
                if last % STEPS == 0:
                    slot = (last // STEPS - 1) * 2 + b
                    sum_s[h, m, pl.ds(slot, 1), :] = cum[SLAB - 1 : SLAB]
                    sum_s[h, m, pl.ds(4 + slot, 1), :] = scaled[SLAB - 1 : SLAB]
        for u, m in enumerate(units):
            before_v[h, m] = jnp.dot(tri_v[1], split_v[u, 1], preferred_element_type=F32)
            tail_v[h, m] = jnp.dot(tri_v[2], split_v[u, 2], preferred_element_type=F32)
        for u, m in enumerate(units):
            for s in range(SEQS):
                for b in range(2):
                    slot = s * 2 + b
                    lanes = pl.ds(b * HALF, HALF)
                    before = before_v[h, m, pl.ds(s * STEPS + STEPS - 1, 1), lanes]
                    end = sum_s[h, m, pl.ds(slot, 1), :]
                    held = sum_s[h, m, pl.ds(4 + slot, 1), :]
                    sum_s[h, m, pl.ds(4 + slot, 1), :] = end * (before + held)
                    sum_s[h, m, pl.ds(8 + slot, 1), :] = tail_v[h, m, pl.ds(s * STEPS, 1), lanes]

    def factors(h):
        def body(m, carry):
            for b, rows, lanes in slabs():
                k = 2 * m + b
                at = (h, m, rows, lanes)
                rate = rate_v[0:1, pl.ds(pl.multiple_of(k * BW + h * HALF, HALF), HALF)]
                values = x_v[k, rows, pl.ds(h * HALF, HALF)].astype(F32)
                recur, inject, decay = f_v[at], q3_v[at], e_v[at]
                e = (rate_gain * recur) * decay
                e_v[at] = e
                c_v[at] = e * decay * (inject * values) * c_v[at]
                f_v[at] = rate * (1.0 - recur)
                q4 = q4_v[at] * inject
                q4_v[at] = q4
                q3_v[at] = q4 * values * (1.0 - inject)
            return carry

        lax.fori_loop(0, PAIRS, body, 0)

    def remote(src, dst, send, recv, target):
        return pltpu.make_async_remote_copy(
            src_ref=src, dst_ref=dst, send_sem=send, recv_sem=recv,
            device_id=target, device_id_type=pl.DeviceIdType.MESH,
        )

    def in_group(source, landing, send, recv, peer):
        return remote(source.at[peer], landing.at[member], send, recv, device(y, z, peer))

    def along(axis, landing, send, recv, peer):
        here = z if axis == "z" else y
        target = device(y, peer, member) if axis == "z" else device(peer, z, member)
        return remote(landing.at[here], landing.at[here], send, recv, target)

    def all_of(landing, send, recv, count):
        every = landing.at[pl.ds(0, count - 1)]
        return remote(every, every, send, recv, device(y, z, x * NC + (1 - core)))

    def group_all(source, landing, send, recv):
        return all_of(landing, send, recv, GROUP)

    def along_all(axis, landing, send, recv):
        return all_of(landing, send, recv, SIZES[axis])

    def far_first(size):
        return sorted(range(1, size), key=lambda step: -min(step, size - step))

    def group_peers():
        return [lax.rem(member + step, GROUP) for step in far_first(GROUP)]

    def axis_peers(axis):
        here, size = (z, NZ) if axis == "z" else (y, NY)
        return [lax.rem(here + step, size) for step in far_first(size)]

    mult, first, back = pl.ds(0, 4), pl.ds(4, 4), pl.ds(8, 4)
    ones, zeros = jnp.ones((4, 128), F32), jnp.zeros((4, 128), F32)

    def total_of(ref, count):
        decay = ref[0, mult]
        state = ref[0, first]
        for j in range(1, count):
            state = ref[j, mult] * state + ref[j, first]
            decay = decay * ref[j, mult]
        adjoint = ref[count - 1, back]
        for j in range(count - 2, -1, -1):
            adjoint = ref[j, mult] * adjoint + ref[j, back]
        return decay, state, adjoint

    def put(ref, index, values):
        for position, value in enumerate(values):
            ref[index, pl.ds(4 * position, 4)] = value
        ref[index, pl.ds(12, 4)] = zeros

    def earlier(ref, count, position, decay, state):
        for j in range(count):
            use = j < position
            state = jnp.where(use, ref[j, mult] * state + ref[j, first], state)
            decay = jnp.where(use, ref[j, mult] * decay, decay)
        return decay, state

    def later(ref, count, position, decay, adjoint):
        for j in range(count - 1, -1, -1):
            use = j > position
            adjoint = jnp.where(use, ref[j, mult] * adjoint + ref[j, back], adjoint)
            decay = jnp.where(use, ref[j, mult] * decay, decay)
        return decay, adjoint

    def group_1(h):
        return sum_s.at[h], sum_r.at[h], g1_send.at[h], g1_recv.at[h]

    def group_2(h):
        return ent_s.at[h], ent_r.at[h], g2_send.at[h], g2_recv.at[h]

    def along_z(h):
        return "z", zsum_r.at[h], z1_send.at[h], z1_recv.at[h]

    def along_y(h):
        return "y", ysum_r.at[h], y1_send.at[h], y1_recv.at[h]

    def local_turns(h, stop):
        def body(turn, carry):
            chip = chip_at(turn)
            local(h, chip)
            for c in range(NC):
                in_group(*group_1(h), chip * NC + c).start()
            return carry

        lax.fori_loop(0, stop, body, 0)

    def last_turn(h):
        local(h, x)
        in_group(*group_1(h), x * NC + (1 - core)).start()
        sum_r[h, member] = sum_s[h, member]

    def to_z(h):
        group_all(*group_1(h)).wait_recv()
        put(zsum_r.at[h], z, total_of(sum_r.at[h], GROUP))
        for peer in axis_peers("z"):
            along(*along_z(h), peer).start()

    def to_y(h):
        along_all(*along_z(h)).wait_recv()
        put(ysum_r.at[h], y, total_of(zsum_r.at[h], NZ))
        for peer in axis_peers("y"):
            along(*along_y(h), peer).start()

    def to_members(h):
        z_decay, z_state = earlier(zsum_r.at[h], NZ, z, ones, zeros)
        z_fade, z_adjoint = later(zsum_r.at[h], NZ, z, ones, zeros)
        along_all(*along_y(h)).wait_recv()
        state = z_decay * earlier(ysum_r.at[h], NY, y, ones, zeros)[1] + z_state
        adjoint = z_fade * later(ysum_r.at[h], NY, y, ones, zeros)[1] + z_adjoint
        for j in range(GROUP):
            ent_s[h, j, pl.ds(0, 4)] = state
            state = sum_r[h, j, mult] * state + sum_r[h, j, first]
        for j in range(GROUP - 1, -1, -1):
            ent_s[h, j, pl.ds(4, 4)] = adjoint
            adjoint = sum_r[h, j, mult] * adjoint + sum_r[h, j, back]
        for peer in group_peers():
            in_group(*group_2(h), peer).start()
        ent_r[h, member] = ent_s[h, member]

    def entered(h):
        group_all(*group_2(h)).wait_recv()

    def summaries_sent():
        for h in range(2):
            group_all(*group_1(h)).wait_send()
            group_all(*group_2(h)).wait_send()
            along_all(*along_z(h)).wait_send()
            along_all(*along_y(h)).wait_send()

    other = device(y, z, x * NC + (1 - core))

    def core_copy(h, m):
        high, low = m // 4, pl.ds(2 * lax.rem(m, 4), 2)
        return remote(
            grad_v.at[h, :, high, low, :, 1 - core], part_v.at[h, :, high, low],
            core_send.at[h], core_recv.at[h], other,
        )

    def core_all(h):
        return remote(part_v.at[h], part_v.at[h], core_send.at[h], core_recv.at[h], other)

    def gradient(h, step):
        units = [2 * step, 2 * step + 1]
        for m in units:
            for b in range(2):
                k = 2 * m + b
                lanes = pl.ds(b * HALF, HALF)
                sums = [jnp.zeros((8, 128), F32) for _ in range(3)]
                for s in range(SEQS):
                    slot = s * 2 + b
                    entering = ent_r[h, m, pl.ds(slot, 1), :]
                    arriving = ent_r[h, m, pl.ds(4 + slot, 1), :] * sum_s[h, m, pl.ds(slot, 1), :]
                    for top in range(s * STEPS, (s + 1) * STEPS, SLAB):
                        rows = pl.ds(top, SLAB)
                        at = (h, m, rows, lanes)
                        adj = inv_v[at] * (tail_v[at] + arriving)
                        previous = pex_v[at] * (before_v[at] + entering)
                        rated = adj * (c_v[at] - previous * e_v[at])
                        pre_r = rated * f_v[at]
                        pre_i = adj * q3_v[at]
                        dg_v[at] = adj * q4_v[at]
                        p_v[k, h, rows, pl.ds(0, HALF)] = pre_r.astype(BF16)
                        p_v[k, h, rows, pl.ds(HALF, HALF)] = pre_i.astype(BF16)
                        for position, value in enumerate((pre_r, pre_i, rated)):
                            for part in range(0, SLAB, 8):
                                sums[position] = sums[position] + value[part : part + 8]
                for position in range(3):
                    line = position * 4 + h * 2 + b
                    vec_s[m, pl.ds(line, 1), :] = jnp.sum(sums[position], axis=0, keepdims=True)
        for m in units:
            for b in range(2):
                k = 2 * m + b
                outer = lax.dot_general(
                    x_v[k], p_v[k, h], (((0,), (0,)), ((), ())), preferred_element_type=F32
                )
                for g in range(2):
                    grad_v[h, g, m // 4, 2 * lax.rem(m, 4) + b] = outer[
                        :, g * HALF : (g + 1) * HALF
                    ].reshape(NX, NC, 32, HALF)
            core_copy(h, m).start()

    def gradient_steps(h, start, stop):
        def body(step, carry):
            gradient(h, step)
            return carry

        lax.fori_loop(start, stop, body, 0)

    def out_copy(k):
        lanes = pl.ds(pl.multiple_of(k * BW, BW), BW)
        return pltpu.make_async_copy(out_v.at[k], out_hbm.at[:, lanes], out_sem)

    def through(quarter):
        def body(m, carry):
            for b in range(2):
                k = 2 * m + b
                across = (((1,), (1,)), ((), ()))
                for h in range(2):
                    back_in = lax.dot_general(
                        p_v[k, h], gate_columns(k, h), across, preferred_element_type=F32
                    )
                    total = back_in if h == 0 else total + back_in
                for h in range(2):
                    mine = pl.ds(h * HALF, HALF)
                    direct = dg_v[h, m, :, pl.ds(b * HALF, HALF)]
                    out_v[k, :, mine] = (direct + total[:, h * HALF : (h + 1) * HALF]).astype(BF16)
                out_copy(k).start()
            return carry

        lax.fori_loop(2 * quarter, 2 * quarter + 2, body, 0)

    def core_sum(h):
        core_all(h).wait_recv()

        def body(m, carry):
            high = m // 4
            for g in range(2):
                for b in range(2):
                    at = 2 * lax.rem(m, 4) + b
                    part_v[h, g, high, at] = part_v[h, g, high, at] + grad_v[h, g, high, at, :, core]
            return carry

        lax.fori_loop(0, PAIRS, body, 0)

    here = {"y": y, "z": z, "x": x}

    def index_of(axis, at, whole, halved, side):
        if not whole:
            return (at // 2, lax.rem(at, 2)) if axis == "y" else (at,)
        if axis == "y":
            return (pl.ds(side, 1) if halved else pl.ds(0, 2), pl.ds(0, 2))
        size = SIZES[axis]
        return (pl.ds(side * (size // 2), size // 2) if halved else pl.ds(0, size),)

    def view(h, part, stage, target, halved, side):
        row0, rows, order = PARTS[h][part]
        axis, axes = order[stage], free_axes(order, stage)
        found = (h,)
        for name in "yzx":
            if name == axis:
                found += index_of(name, target, False, False, 0)
            elif name in axes:
                found += index_of(name, 0, True, halved and name == axes[0], side)
            else:
                found += index_of(name, here[name], False, False, 0)
        return found + (pl.ds(row0, rows), slice(None))

    def far_all(h, part, number):
        buffer = landing[LANDING[h, part, number]]
        axis, step = rounds_of(PARTS[h][part][2])[number][1:]
        every = buffer if step > 0 else buffer.at[pl.ds(0, SIZES[axis] - 1)]
        at = LANDING[h, part, number]
        return remote(every, every, far_send.at[at], far_recv.at[at], other)

    def ring_copy(h, part, number, side):
        stage, axis, step = rounds_of(PARTS[h][part][2])[number]
        size = SIZES[axis]
        half = size // 2
        sent = here[axis] + (half - step + 1 if side == 0 else size - half + step - 1)
        place = dict(here)
        place[axis] = lax.rem(here[axis] + (1 if side == 0 else size - 1), size)
        at = LANDING[h, part, number]
        return remote(
            part_v.at[view(h, part, stage, lax.rem(sent, size), step == 1, side)],
            landing[LANDING[h, part, number]].at[side], far_send.at[at], far_recv.at[at],
            device(place["y"], place["z"], place["x"] * NC + core),
        )

    def direct_copy(h, part, number, peer):
        stage, axis, _ = rounds_of(PARTS[h][part][2])[number]
        place = dict(here)
        place[axis] = peer
        at = LANDING[h, part, number]
        return remote(
            part_v.at[view(h, part, stage, peer, False, 0)],
            landing[LANDING[h, part, number]].at[here[axis]], far_send.at[at], far_recv.at[at],
            device(place["y"], place["z"], place["x"] * NC + core),
        )

    def copies_out(h, part, number):
        _, axis, step = rounds_of(PARTS[h][part][2])[number]
        if step > 0:
            return [ring_copy(h, part, number, side) for side in range(2)]
        peers = [lax.rem(here[axis] + far, SIZES[axis]) for far in far_first(SIZES[axis])]
        return [direct_copy(h, part, number, peer) for peer in peers]

    def far_start(h, part, number):
        for copy in copies_out(h, part, number):
            copy.start()

    def add_landed(at, axes, halved, side, buffer, slots):
        if len(axes) == 0:
            part_v[at] = part_v[at] + sum(buffer[slot] for slot in slots)
            return
        axis = axes[0]
        size = SIZES[axis] // 2 if halved else SIZES[axis]
        position = 1 + {"y": 0, "z": 2, "x": 3}[axis]
        width = 2 if axis == "y" else 1
        base = size * side if halved else 0

        def body(i, carry):
            if axis == "y":
                from_, to = (i // 2, lax.rem(i, 2)), ((base + i) // 2, lax.rem(base + i, 2))
            else:
                from_, to = (i,), (base + i,)
            place = at[:position] + to + at[position + width :]
            part_v[place] = part_v[place] + sum(buffer[(slot,) + from_] for slot in slots)
            return carry

        lax.fori_loop(0, size, body, 0)

    def far_finish(h, part, number):
        order = PARTS[h][part][2]
        stage, axis, step = rounds_of(order)[number]
        size, axes = SIZES[axis], free_axes(order, stage)
        buffer = landing[LANDING[h, part, number]]
        far_all(h, part, number).wait_recv()
        if step == 0:
            peers = [lax.rem(here[axis] + far, size) for far in range(1, size)]
            at = view(h, part, stage, here[axis], False, 0)
            add_landed(at, axes, False, 0, buffer, peers)
            return
        half = size // 2
        for side in range(2):
            came = here[axis] + (half - step if side == 0 else size - half + step)
            at = view(h, part, stage, lax.rem(came, size), step == 1, side)
            add_landed(at, axes, step == 1, side, buffer, [side])

    vector_1 = (vec_s, vec_r, v1_send, v1_recv)
    vector_z = ("z", vecz_r, vz_send, vz_recv)
    vector_y = ("y", vecy_r, vy_send, vy_recv)

    vector_2 = (veco_r, veco_r, v2_send, v2_recv)

    def vector_copy(peer):
        return remote(veco_r.at[member], veco_r.at[member], v2_send, v2_recv, device(y, z, peer))

    def vector_out():
        for peer in group_peers():
            in_group(*vector_1, peer).start()
        vec_r[member] = vec_s[member]

    def vector_step(step):
        if step == 0:
            group_all(*vector_1).wait_recv()
            vecz_r[z] = sum(vec_r[j] for j in range(GROUP))
            for peer in axis_peers("z"):
                along(*vector_z, peer).start()
        elif step == 1:
            along_all(*vector_z).wait_recv()
            vecy_r[y] = sum(vecz_r[j] for j in range(NZ))
            for peer in axis_peers("y"):
                along(*vector_y, peer).start()
        elif step == 2:
            along_all(*vector_y).wait_recv()
            veco_r[member] = sum(vecy_r[j] for j in range(NY))
            for peer in group_peers():
                vector_copy(peer).start()
        else:
            group_all(*vector_2).wait_recv()
            for j in range(GROUP):
                for position in range(3):
                    for h in range(2):
                        for b in range(2):
                            lanes = pl.ds((2 * j + b) * BW + h * HALF, HALF)
                            line = veco_r[j, pl.ds(position * 4 + h * 2 + b, 1), :]
                            if position < 2:
                                bg_ref[pl.ds(position, 1), lanes] = line
                            else:
                                rg_ref[:, lanes] = line

    pl.semaphore_wait(barrier, (GROUP - 1) + (NZ - 1) + (NY - 1))
    local_turns(0, NX - 1)
    last_turn(0)
    local_turns(1, NX - 1)
    to_z(0)
    last_turn(1)
    factors(0)
    to_y(0)
    to_z(1)
    factors(1)
    to_members(0)
    to_y(1)
    entered(0)
    gradient_steps(0, 0, 2)
    to_members(1)
    gradient_steps(0, 2, 4)
    core_sum(0)
    for part in range(3):
        far_start(0, part, 0)
    entered(1)
    gradient_steps(1, 0, 4)
    vector_out()
    core_sum(1)
    for part in range(3):
        far_start(1, part, 0)
    for event in EVENTS:
        if isinstance(event, str):
            kind, number = event.split()
            (through if kind == "through" else vector_step)(int(number))
            continue
        h, part, number = event
        far_finish(h, part, number)
        if number + 1 < len(rounds_of(PARTS[h][part][2])):
            far_start(h, part, number + 1)
    for h in range(2):
        gg_ref[:, pl.ds(h * HALF, HALF)] = part_v[h, y // 2, lax.rem(y, 2), z, x]

    summaries_sent()
    group_all(*vector_1).wait_send()
    group_all(*vector_2).wait_send()
    along_all(*vector_z).wait_send()
    along_all(*vector_y).wait_send()
    for h, part, number in LANDING:
        far_all(h, part, number).wait_send()
    for h in range(2):
        core_all(h).wait_send()
    pltpu.make_async_copy(out_v, out_v, out_sem).wait()


def finish(*refs):
    sources, results, held, sem = refs[:4], refs[4:8], refs[8:12], refs[12]
    count = 0
    pairs = []
    for source, result, hold in zip(sources, results, held):
        rows = source.shape[0]
        size = 16 if rows == ROWS else rows
        for top in range(0, rows, size):
            at = pl.ds(top, size)
            pairs.append((
                pltpu.make_async_copy(source.at[at], hold.at[at], sem.at[0, count]),
                pltpu.make_async_copy(hold.at[at], result.at[at], sem.at[1, count]),
            ))
            count += 1
    for into, _ in pairs:
        into.start()
    for into, out in pairs:
        into.wait()
        out.start()
    for _, out in pairs:
        out.wait()


def per_device(inputs, grad_out, gate_weights, gate_biases, decay_rate):
    shape = inputs.shape
    hbm = pl.BlockSpec(memory_space=pl.ANY)
    vmem = pl.BlockSpec(memory_space=pltpu.VMEM)
    dma = pltpu.SemaphoreType.DMA
    block32 = pltpu.VMEM((2, PAIRS, ROWS, BW), F32)
    block16 = pltpu.VMEM((BLOCKS, ROWS, BW), BF16)
    unit32 = pltpu.VMEM((2, ROWS, BW), F32)
    scratch = [
        block16, block16, pltpu.VMEM((2, BLOCKS, BW, BW), BF16),
        pltpu.VMEM((2, D), F32), pltpu.VMEM((1, D), F32), block16,
        pltpu.VMEM((3, ROWS, 2 * ROWS), BF16), pltpu.VMEM((2, 2, ROWS, BW), F32),
        unit32, unit32, unit32, pltpu.VMEM((2, 3, 2 * ROWS, BW), BF16),
        block32, pltpu.VMEM((BLOCKS, 2, ROWS, BW), BF16),
    ]
    scratch += [block32] * 9
    scratch += [
        pltpu.VMEM((2, GROUP, 16, 128), F32), pltpu.VMEM((2, GROUP, 16, 128), F32),
        pltpu.VMEM((2, NZ, 16, 128), F32), pltpu.VMEM((2, NY, 16, 128), F32),
        pltpu.VMEM((2, GROUP, 8, 128), F32), pltpu.VMEM((2, GROUP, 8, 128), F32),
        pltpu.VMEM((GROUP, 16, 128), F32), pltpu.VMEM((GROUP, 16, 128), F32),
        pltpu.VMEM((NZ, 16, 128), F32), pltpu.VMEM((NY, 16, 128), F32),
        pltpu.VMEM((GROUP, 16, 128), F32),
        pltpu.VMEM((2, 2, 2, NZ, NX, NC, 32, HALF), F32),
        pltpu.VMEM((2, 2, 2, NZ, NX, 32, HALF), F32),
        dma((3, 4)), dma((2,)), dma(()),
        dma((2,)), dma((2,)), dma((2,)), dma((2,)), dma((2,)), dma((2,)), dma((2,)), dma((2,)),
        dma(()), dma(()), dma(()), dma(()), dma(()), dma(()), dma(()), dma(()),
        dma((2,)), dma((2,)), dma((len(LANDING),)), dma((len(LANDING),)),
    ]
    scratch += [pltpu.VMEM(found, F32) for found in LANDING_SHAPES]
    shapes = (
        jax.ShapeDtypeStruct((ROWS, D), BF16),
        jax.ShapeDtypeStruct((32, BW), F32),
        jax.ShapeDtypeStruct((2, D), F32),
        jax.ShapeDtypeStruct((1, D), F32),
    )
    results = pl.pallas_call(
        kernel,
        out_shape=shapes,
        in_specs=[hbm] * 5,
        out_specs=(hbm, vmem, vmem, vmem),
        scratch_shapes=scratch,
        compiler_params=pltpu.CompilerParams(
            collective_id=0, has_side_effects=True, vmem_limit_bytes=60 * 2**20
        ),
    )(
        inputs.reshape(ROWS, D), grad_out.reshape(ROWS, D), gate_weights,
        gate_biases, decay_rate.reshape(1, D),
    )
    input_grad, gate_grads, bias_grads, rate_grad = pl.pallas_call(
        finish, out_shape=shapes, in_specs=[hbm] * 4, out_specs=[hbm] * 4,
        scratch_shapes=[pltpu.VMEM(found.shape, found.dtype) for found in shapes] + [dma((2, 11))],
    )(*results)
    return (input_grad.reshape(shape), gate_grads, bias_grads, rate_grad.reshape(D))


def solution(mesh):
    in_specs = (P(None, ("outer", "inner"), None), P(None, ("outer", "inner"), None), P(), P(), P())
    out_specs = (P(None, ("outer", "inner"), None), P(("outer", "inner"), None), P(), P())
    return jax.shard_map(
        per_device, mesh=mesh, in_specs=in_specs, out_specs=out_specs, check_vma=False
    )
```

```python
import functools

import jax
import jax.numpy as jnp
from jax import lax
from jax.experimental import pallas as pl
from jax.experimental.pallas import tpu as pltpu
from jax.sharding import PartitionSpec as P

F32, BF16 = jnp.float32, jnp.bfloat16
rate_gain = 8.0
NY, NZ, NX, NC = 4, 8, 4, 2
GROUP = NX * NC
BLOCKS, BW, D = 16, 256, 4096
SEQS, STEPS = 2, 64
ROWS = SEQS * STEPS
PAIRS = BLOCKS // 2
SLAB = 32
SIZES = {"y": NY, "z": NZ, "x": NX}

HALF = BW // 2

PARTS = (
    ((0, 16, "zyx"), (16, 8, "zxy"), (24, 8, "yxz")),
    ((0, 16, "xyz"), (16, 8, "yxz"), (24, 8, "yxz")),
)


def rounds_of(order):
    rounds = []
    for stage, axis in enumerate(order):
        if stage == 0:
            rounds += [(stage, axis, step) for step in range(1, SIZES[axis] // 2 + 1)]
        else:
            rounds.append((stage, axis, 0))
    return rounds


def free_axes(order, stage):
    return [axis for axis in "yzx" if axis in order[stage + 1 :]]


def lead_shape(axes, halved):
    shape = []
    for position, axis in enumerate(axes):
        half = halved and position == 0
        if axis == "y":
            shape += [1 if half else 2, 2]
        else:
            shape += [SIZES[axis] // 2 if half else SIZES[axis]]
    return tuple(shape)


def landing_buffers():
    places, shapes = {}, []
    for h in range(2):
        for part, (_, rows, order) in enumerate(PARTS[h]):
            for number, (stage, axis, step) in enumerate(rounds_of(order)):
                count = SIZES[axis] if step == 0 else 2
                places[h, part, number] = len(shapes)
                lead = lead_shape(free_axes(order, stage), step == 1)
                shapes.append((count,) + lead + (rows, HALF))
    return places, shapes


LANDING, LANDING_SHAPES = landing_buffers()

EVENTS = [
    (0, 0, 0), (0, 2, 0), (0, 1, 0), "through 0", "through 1", "through 2", (0, 0, 1), (0, 2, 1),
    "vector 0", (0, 1, 1), (1, 0, 0), (1, 1, 0), (1, 2, 0), "through 3", (0, 2, 2), (0, 0, 2),
    "vector 1", (0, 1, 2), (1, 1, 1), (1, 0, 1), (1, 2, 1), "vector 2", (0, 2, 3), (0, 0, 3),
    (1, 1, 2), (0, 1, 3), "vector 3", (1, 2, 2), (1, 0, 2), (0, 0, 4), (0, 1, 4), (1, 1, 3),
    (1, 2, 3), (0, 0, 5), (0, 1, 5), (1, 0, 3),
]


def kernel(
    x_hbm, go_hbm, w_hbm, bias_hbm, rate_hbm,
    out_hbm, gg_ref, bg_ref, rg_ref,
    x_v, go_v, w_v, bias_v, rate_v, out_v,
    tri_v, pre_v, drive_v, lc_v, split_v, dg_v, p_v,
    inv_v, cum_v, before_v, tail_v, c_v, e_v, f_v, q3_v, q4_v,
    sum_s, sum_r, zsum_r, ysum_r, ent_s, ent_r,
    vec_s, vec_r, vecz_r, vecy_r, veco_r,
    grad_v, part_v,
    in_sem, small_sem, out_sem,
    g1_send, g1_recv, z1_send, z1_recv, y1_send, y1_recv, g2_send, g2_recv,
    v1_send, v1_recv, vz_send, vz_recv, vy_send, vy_recv, v2_send, v2_recv,
    core_send, core_recv, far_send, far_recv,
    *landing,
):
    y = lax.axis_index("outer")
    inner = lax.axis_index("inner")
    z = inner // GROUP
    member = lax.rem(inner, GROUP)
    x = member // NC
    core = lax.rem(member, NC)

    def device(y_at, z_at, member_at):
        return (y_at, z_at * GROUP + member_at)

    barrier = pltpu.get_barrier_semaphore()

    def greet(target):
        pl.semaphore_signal(barrier, inc=1, device_id=target, device_id_type=pl.DeviceIdType.MESH)

    for step in range(1, GROUP):
        greet(device(y, z, lax.rem(member + step, GROUP)))
    for step in range(1, NZ):
        greet(device(y, lax.rem(z + step, NZ), member))
    for step in range(1, NY):
        greet(device(lax.rem(y + step, NY), z, member))

    def chip_at(turn):
        return lax.rem(x + 1 + turn, NX)

    def start_loads(turn, carry):
        step = chip_at(turn)
        blocks = pl.ds(4 * step, 4)
        for b in range(4):
            k = 4 * step + b
            lanes = pl.ds(pl.multiple_of(k * BW, BW), BW)
            pltpu.make_async_copy(x_hbm.at[:, lanes], x_v.at[k], in_sem.at[0, step]).start()
        pltpu.make_async_copy(w_hbm.at[:, blocks], w_v.at[:, blocks], in_sem.at[1, step]).start()
        for b in range(4):
            k = 4 * step + b
            lanes = pl.ds(pl.multiple_of(k * BW, BW), BW)
            pltpu.make_async_copy(go_hbm.at[:, lanes], go_v.at[k], in_sem.at[2, step]).start()
        return carry

    def wait_loads(step):
        blocks = pl.ds(4 * step, 4)
        pltpu.make_async_copy(x_v.at[blocks], x_v.at[blocks], in_sem.at[0, step]).wait()
        pltpu.make_async_copy(w_hbm.at[:, blocks], w_v.at[:, blocks], in_sem.at[1, step]).wait()
        pltpu.make_async_copy(go_v.at[blocks], go_v.at[blocks], in_sem.at[2, step]).wait()

    bias_copy = pltpu.make_async_copy(bias_hbm, bias_v, small_sem.at[0])
    rate_copy = pltpu.make_async_copy(rate_hbm, rate_v, small_sem.at[1])
    bias_copy.start()
    rate_copy.start()
    lax.fori_loop(0, 4, start_loads, 0)

    row = lax.broadcasted_iota(jnp.int32, (ROWS, 2 * ROWS), 0)
    col = lax.broadcasted_iota(jnp.int32, (ROWS, 2 * ROWS), 1)
    col = jnp.where(col >= ROWS, col - ROWS, col)
    same = jnp.where(row >= STEPS, 1, 0) == jnp.where(col >= STEPS, 1, 0)
    tri_v[0] = jnp.where(same & (col <= row), 1.0, 0.0).astype(BF16)
    tri_v[1] = jnp.where(same & (col < row), 1.0, 0.0).astype(BF16)
    tri_v[2] = jnp.where(same & (col >= row), 1.0, 0.0).astype(BF16)

    vec_s[...] = jnp.zeros_like(vec_s)
    sum_s[...] = jnp.zeros_like(sum_s)
    bias_copy.wait()
    rate_copy.wait()

    def slabs():
        for b in range(2):
            for top in range(0, ROWS, SLAB):
                yield b, pl.ds(top, SLAB), pl.ds(b * HALF, HALF)

    def split_store(u, which, top, lanes, value):
        high = value.astype(BF16)
        split_v[u, which, pl.ds(top, SLAB), lanes] = high
        split_v[u, which, pl.ds(ROWS + top, SLAB), lanes] = (value - high.astype(F32)).astype(BF16)

    def gate_columns(k, h):
        lanes = pl.ds(h * HALF, HALF)
        return jnp.concatenate([w_v[0, k, :, lanes], w_v[1, k, :, lanes]], axis=1)

    def local(h, step):
        mine = pl.ds(h * HALF, HALF)
        units = [2 * step, 2 * step + 1]
        if h == 0:
            wait_loads(step)
        for u, m in enumerate(units):
            for b in range(2):
                k = 2 * m + b
                pre_v[u, b] = jnp.dot(x_v[k], gate_columns(k, h), preferred_element_type=F32)
        for u, m in enumerate(units):
            for b, rows, lanes in slabs():
                k = 2 * m + b
                column = pl.ds(pl.multiple_of(k * BW + h * HALF, HALF), HALF)
                rate = rate_v[0:1, column]
                pre_r = pre_v[u, b, rows, pl.ds(0, HALF)] + bias_v[0:1, column]
                pre_i = pre_v[u, b, rows, pl.ds(HALF, HALF)] + bias_v[1:2, column]
                recur = 1.0 / (1.0 + jnp.exp(-pre_r))
                inject = 1.0 / (1.0 + jnp.exp(-pre_i))
                values = x_v[k, rows, mine].astype(F32)
                log_decay = (-rate_gain * rate) * recur
                decay = jnp.exp(log_decay)
                series = -log_decay * (
                    1.0 + log_decay * (0.5 + log_decay * (1.0 / 6.0 + log_decay * (1.0 / 24.0)))
                )
                lost = jnp.where(log_decay > -0.1, series, 1.0 - decay)
                square = lost * (1.0 + decay)
                inverse_scale = lax.rsqrt(square)
                scale = square * inverse_scale
                driven = inject * values
                drive_v[u, rows, lanes] = scale * driven
                split_store(u, 0, rows.start, lanes, log_decay)
                at = (h, m, rows, lanes)
                e_v[at], c_v[at], f_v[at] = decay, inverse_scale, recur
                q4_v[at], q3_v[at] = scale, inject
        for u, m in enumerate(units):
            lc_v[u] = jnp.dot(tri_v[0], split_v[u, 0], preferred_element_type=F32)
        for u, m in enumerate(units):
            for b, rows, lanes in slabs():
                log_cum = lc_v[u, rows, lanes]
                cum = jnp.exp(log_cum)
                inverse = jnp.exp(-log_cum)
                inv_v[h, m, rows, lanes] = inverse
                cum_v[h, m, rows, lanes] = cum
                scaled = drive_v[u, rows, lanes] * inverse
                split_store(u, 1, rows.start, lanes, scaled)
                upstream = go_v[2 * m + b, rows, mine].astype(F32)
                split_store(u, 2, rows.start, lanes, cum * upstream)
                last = rows.start + SLAB
                if last % STEPS == 0:
                    slot = (last // STEPS - 1) * 2 + b
                    sum_s[h, m, pl.ds(slot, 1), :] = cum[SLAB - 1 : SLAB]
                    sum_s[h, m, pl.ds(4 + slot, 1), :] = scaled[SLAB - 1 : SLAB]
        for u, m in enumerate(units):
            before_v[h, m] = jnp.dot(tri_v[1], split_v[u, 1], preferred_element_type=F32)
            tail_v[h, m] = jnp.dot(tri_v[2], split_v[u, 2], preferred_element_type=F32)
        for u, m in enumerate(units):
            for s in range(SEQS):
                for b in range(2):
                    slot = s * 2 + b
                    lanes = pl.ds(b * HALF, HALF)
                    before = before_v[h, m, pl.ds(s * STEPS + STEPS - 1, 1), lanes]
                    end = sum_s[h, m, pl.ds(slot, 1), :]
                    held = sum_s[h, m, pl.ds(4 + slot, 1), :]
                    sum_s[h, m, pl.ds(4 + slot, 1), :] = end * (before + held)
                    sum_s[h, m, pl.ds(8 + slot, 1), :] = tail_v[h, m, pl.ds(s * STEPS, 1), lanes]

    def factors(h):
        def body(m, carry):
            for b, rows, lanes in slabs():
                k = 2 * m + b
                at = (h, m, rows, lanes)
                rate = rate_v[0:1, pl.ds(pl.multiple_of(k * BW + h * HALF, HALF), HALF)]
                values = x_v[k, rows, pl.ds(h * HALF, HALF)].astype(F32)
                recur, inject, decay = f_v[at], q3_v[at], e_v[at]
                e = rate_gain * recur
                e_v[at] = e
                c_v[at] = e * (decay * decay) * (inject * values) * c_v[at]
                f_v[at] = rate * (1.0 - recur)
                q4 = q4_v[at] * inject
                q4_v[at] = q4
                q3_v[at] = q4 * values * (1.0 - inject)
            return carry

        lax.fori_loop(0, PAIRS, body, 0)

    def remote(src, dst, send, recv, target):
        return pltpu.make_async_remote_copy(
            src_ref=src, dst_ref=dst, send_sem=send, recv_sem=recv,
            device_id=target, device_id_type=pl.DeviceIdType.MESH,
        )

    def in_group(source, landing, send, recv, peer):
        return remote(source.at[peer], landing.at[member], send, recv, device(y, z, peer))

    def along(axis, landing, send, recv, peer):
        here = z if axis == "z" else y
        target = device(y, peer, member) if axis == "z" else device(peer, z, member)
        return remote(landing.at[here], landing.at[here], send, recv, target)

    def all_of(landing, send, recv, count):
        every = landing.at[pl.ds(0, count - 1)]
        return remote(every, every, send, recv, device(y, z, x * NC + (1 - core)))

    def group_all(source, landing, send, recv):
        return all_of(landing, send, recv, GROUP)

    def along_all(axis, landing, send, recv):
        return all_of(landing, send, recv, SIZES[axis])

    def far_first(size):
        return sorted(range(1, size), key=lambda step: -min(step, size - step))

    def group_peers():
        return [lax.rem(member + step, GROUP) for step in far_first(GROUP)]

    def axis_peers(axis):
        here, size = (z, NZ) if axis == "z" else (y, NY)
        return [lax.rem(here + step, size) for step in far_first(size)]

    mult, first, back = pl.ds(0, 4), pl.ds(4, 4), pl.ds(8, 4)
    ones, zeros = jnp.ones((4, 128), F32), jnp.zeros((4, 128), F32)

    def total_of(ref, count):
        decay = ref[0, mult]
        state = ref[0, first]
        for j in range(1, count):
            state = ref[j, mult] * state + ref[j, first]
            decay = decay * ref[j, mult]
        adjoint = ref[count - 1, back]
        for j in range(count - 2, -1, -1):
            adjoint = ref[j, mult] * adjoint + ref[j, back]
        return decay, state, adjoint

    def put(ref, index, values):
        for position, value in enumerate(values):
            ref[index, pl.ds(4 * position, 4)] = value
        ref[index, pl.ds(12, 4)] = zeros

    def earlier(ref, count, position, decay, state):
        for j in range(count):
            use = j < position
            state = jnp.where(use, ref[j, mult] * state + ref[j, first], state)
            decay = jnp.where(use, ref[j, mult] * decay, decay)
        return decay, state

    def later(ref, count, position, decay, adjoint):
        for j in range(count - 1, -1, -1):
            use = j > position
            adjoint = jnp.where(use, ref[j, mult] * adjoint + ref[j, back], adjoint)
            decay = jnp.where(use, ref[j, mult] * decay, decay)
        return decay, adjoint

    def group_1(h):
        return sum_s.at[h], sum_r.at[h], g1_send.at[h], g1_recv.at[h]

    def group_2(h):
        return ent_s.at[h], ent_r.at[h], g2_send.at[h], g2_recv.at[h]

    def along_z(h):
        return "z", zsum_r.at[h], z1_send.at[h], z1_recv.at[h]

    def along_y(h):
        return "y", ysum_r.at[h], y1_send.at[h], y1_recv.at[h]

    def local_turns(h, start, stop):
        def body(turn, carry):
            chip = chip_at(turn)
            local(h, chip)
            for c in range(NC):
                in_group(*group_1(h), chip * NC + c).start()
            return carry

        lax.fori_loop(start, stop, body, 0)

    def last_turn(h):
        local(h, x)
        in_group(*group_1(h), x * NC + (1 - core)).start()
        sum_r[h, member] = sum_s[h, member]

    def to_z(h):
        group_all(*group_1(h)).wait_recv()
        put(zsum_r.at[h], z, total_of(sum_r.at[h], GROUP))
        for peer in axis_peers("z"):
            along(*along_z(h), peer).start()

    def to_y(h):
        along_all(*along_z(h)).wait_recv()
        put(ysum_r.at[h], y, total_of(zsum_r.at[h], NZ))
        for peer in axis_peers("y"):
            along(*along_y(h), peer).start()

    def to_members(h):
        z_decay, z_state = earlier(zsum_r.at[h], NZ, z, ones, zeros)
        z_fade, z_adjoint = later(zsum_r.at[h], NZ, z, ones, zeros)
        along_all(*along_y(h)).wait_recv()
        state = z_decay * earlier(ysum_r.at[h], NY, y, ones, zeros)[1] + z_state
        adjoint = z_fade * later(ysum_r.at[h], NY, y, ones, zeros)[1] + z_adjoint
        for j in range(GROUP):
            ent_s[h, j, pl.ds(0, 4)] = state
            state = sum_r[h, j, mult] * state + sum_r[h, j, first]
        for j in range(GROUP - 1, -1, -1):
            ent_s[h, j, pl.ds(4, 4)] = adjoint
            adjoint = sum_r[h, j, mult] * adjoint + sum_r[h, j, back]
        for peer in group_peers():
            in_group(*group_2(h), peer).start()
        ent_r[h, member] = ent_s[h, member]

    def entered(h):
        group_all(*group_2(h)).wait_recv()

    def summaries_sent():
        for h in range(2):
            group_all(*group_1(h)).wait_send()
            group_all(*group_2(h)).wait_send()
            along_all(*along_z(h)).wait_send()
            along_all(*along_y(h)).wait_send()

    other = device(y, z, x * NC + (1 - core))

    def core_copy(h, m):
        high, low = m // 4, pl.ds(2 * lax.rem(m, 4), 2)
        return remote(
            grad_v.at[h, :, high, low, :, 1 - core], part_v.at[h, :, high, low],
            core_send.at[h, high], core_recv.at[h, high], other,
        )

    def core_all(h, high):
        every = part_v.at[h, :, high]
        return remote(every, every, core_send.at[h, high], core_recv.at[h, high], other)

    def gradient(h, step):
        units = [2 * step, 2 * step + 1]
        for m in units:
            for b in range(2):
                k = 2 * m + b
                lanes = pl.ds(b * HALF, HALF)
                sums = [jnp.zeros((8, 128), F32) for _ in range(3)]
                for s in range(SEQS):
                    slot = s * 2 + b
                    entering = ent_r[h, m, pl.ds(slot, 1), :]
                    arriving = ent_r[h, m, pl.ds(4 + slot, 1), :] * sum_s[h, m, pl.ds(slot, 1), :]
                    for top in range(s * STEPS, (s + 1) * STEPS, SLAB):
                        rows = pl.ds(top, SLAB)
                        at = (h, m, rows, lanes)
                        adj = inv_v[at] * (tail_v[at] + arriving)
                        carried = cum_v[at] * (before_v[at] + entering)
                        rated = adj * (c_v[at] - carried * e_v[at])
                        pre_r = rated * f_v[at]
                        pre_i = adj * q3_v[at]
                        dg_v[at] = adj * q4_v[at]
                        p_v[k, h, rows, pl.ds(0, HALF)] = pre_r.astype(BF16)
                        p_v[k, h, rows, pl.ds(HALF, HALF)] = pre_i.astype(BF16)
                        for position, value in enumerate((pre_r, pre_i, rated)):
                            for part in range(0, SLAB, 8):
                                sums[position] = sums[position] + value[part : part + 8]
                for position in range(3):
                    line = position * 4 + h * 2 + b
                    vec_s[m, pl.ds(line, 1), :] = jnp.sum(sums[position], axis=0, keepdims=True)
        for m in units:
            for b in range(2):
                k = 2 * m + b
                outer = lax.dot_general(
                    x_v[k], p_v[k, h], (((0,), (0,)), ((), ())), preferred_element_type=F32
                )
                for g in range(2):
                    grad_v[h, g, m // 4, 2 * lax.rem(m, 4) + b] = outer[
                        :, g * HALF : (g + 1) * HALF
                    ].reshape(NX, NC, 32, HALF)
            core_copy(h, m).start()

    def gradients(h, high):
        def body(step, carry):
            gradient(h, 2 * high + step)
            return carry

        lax.fori_loop(0, 2, body, 0)

    def out_copy(k):
        lanes = pl.ds(pl.multiple_of(k * BW, BW), BW)
        return pltpu.make_async_copy(out_v.at[k], out_hbm.at[:, lanes], out_sem)

    def through(quarter):
        def body(m, carry):
            for b in range(2):
                k = 2 * m + b
                across = (((1,), (1,)), ((), ()))
                for h in range(2):
                    back_in = lax.dot_general(
                        p_v[k, h], gate_columns(k, h), across, preferred_element_type=F32
                    )
                    total = back_in if h == 0 else total + back_in
                for h in range(2):
                    mine = pl.ds(h * HALF, HALF)
                    direct = dg_v[h, m, :, pl.ds(b * HALF, HALF)]
                    out_v[k, :, mine] = (direct + total[:, h * HALF : (h + 1) * HALF]).astype(BF16)
                out_copy(k).start()
            return carry

        lax.fori_loop(2 * quarter, 2 * quarter + 2, body, 0)

    def core_sum(h, high):
        core_all(h, high).wait_recv()

        def body(at, carry):
            for g in range(2):
                part_v[h, g, high, at] = part_v[h, g, high, at] + grad_v[h, g, high, at, :, core]
            return carry

        lax.fori_loop(0, NZ, body, 0)

    here = {"y": y, "z": z, "x": x}

    def index_of(axis, at, whole, halved, side):
        if not whole:
            return (at // 2, lax.rem(at, 2)) if axis == "y" else (at,)
        if axis == "y":
            return (pl.ds(side, 1) if halved else pl.ds(0, 2), pl.ds(0, 2))
        size = SIZES[axis]
        return (pl.ds(side * (size // 2), size // 2) if halved else pl.ds(0, size),)

    def view(h, part, stage, target, halved, side):
        row0, rows, order = PARTS[h][part]
        axis, axes = order[stage], free_axes(order, stage)
        found = (h,)
        for name in "yzx":
            if name == axis:
                found += index_of(name, target, False, False, 0)
            elif name in axes:
                found += index_of(name, 0, True, halved and name == axes[0], side)
            else:
                found += index_of(name, here[name], False, False, 0)
        return found + (pl.ds(row0, rows), slice(None))

    def far_all(h, part, number):
        buffer = landing[LANDING[h, part, number]]
        axis, step = rounds_of(PARTS[h][part][2])[number][1:]
        every = buffer if step > 0 else buffer.at[pl.ds(0, SIZES[axis] - 1)]
        at = LANDING[h, part, number]
        return remote(every, every, far_send.at[at], far_recv.at[at], other)

    def ring_copy(h, part, number, side):
        stage, axis, step = rounds_of(PARTS[h][part][2])[number]
        size = SIZES[axis]
        half = size // 2
        sent = here[axis] + (half - step + 1 if side == 0 else size - half + step - 1)
        place = dict(here)
        place[axis] = lax.rem(here[axis] + (1 if side == 0 else size - 1), size)
        at = LANDING[h, part, number]
        return remote(
            part_v.at[view(h, part, stage, lax.rem(sent, size), step == 1, side)],
            landing[LANDING[h, part, number]].at[side], far_send.at[at], far_recv.at[at],
            device(place["y"], place["z"], place["x"] * NC + core),
        )

    def direct_copy(h, part, number, peer):
        stage, axis, _ = rounds_of(PARTS[h][part][2])[number]
        place = dict(here)
        place[axis] = peer
        at = LANDING[h, part, number]
        return remote(
            part_v.at[view(h, part, stage, peer, False, 0)],
            landing[LANDING[h, part, number]].at[here[axis]], far_send.at[at], far_recv.at[at],
            device(place["y"], place["z"], place["x"] * NC + core),
        )

    def copies_out(h, part, number):
        _, axis, step = rounds_of(PARTS[h][part][2])[number]
        if step > 0:
            return [ring_copy(h, part, number, side) for side in range(2)]
        peers = [lax.rem(here[axis] + far, SIZES[axis]) for far in far_first(SIZES[axis])]
        return [direct_copy(h, part, number, peer) for peer in peers]

    def far_start(h, part, number):
        for copy in copies_out(h, part, number):
            copy.start()

    def add_landed(at, axes, halved, side, buffer, slots):
        if len(axes) == 0:
            part_v[at] = part_v[at] + sum(buffer[slot] for slot in slots)
            return
        axis = axes[0]
        size = SIZES[axis] // 2 if halved else SIZES[axis]
        position = 1 + {"y": 0, "z": 2, "x": 3}[axis]
        width = 2 if axis == "y" else 1
        base = size * side if halved else 0

        def body(i, carry):
            if axis == "y":
                from_, to = (i // 2, lax.rem(i, 2)), ((base + i) // 2, lax.rem(base + i, 2))
            else:
                from_, to = (i,), (base + i,)
            place = at[:position] + to + at[position + width :]
            part_v[place] = part_v[place] + sum(buffer[(slot,) + from_] for slot in slots)
            return carry

        lax.fori_loop(0, size, body, 0)

    def far_finish(h, part, number):
        order = PARTS[h][part][2]
        stage, axis, step = rounds_of(order)[number]
        size, axes = SIZES[axis], free_axes(order, stage)
        buffer = landing[LANDING[h, part, number]]
        far_all(h, part, number).wait_recv()
        if step == 0:
            peers = [lax.rem(here[axis] + far, size) for far in range(1, size)]
            at = view(h, part, stage, here[axis], False, 0)
            add_landed(at, axes, False, 0, buffer, peers)
            return
        half = size // 2
        for side in range(2):
            came = here[axis] + (half - step if side == 0 else size - half + step)
            at = view(h, part, stage, lax.rem(came, size), step == 1, side)
            add_landed(at, axes, step == 1, side, buffer, [side])

    vector_1 = (vec_s, vec_r, v1_send, v1_recv)
    vector_z = ("z", vecz_r, vz_send, vz_recv)
    vector_y = ("y", vecy_r, vy_send, vy_recv)

    vector_2 = (veco_r, veco_r, v2_send, v2_recv)

    def vector_copy(peer):
        return remote(veco_r.at[member], veco_r.at[member], v2_send, v2_recv, device(y, z, peer))

    def vector_out():
        for peer in group_peers():
            in_group(*vector_1, peer).start()
        vec_r[member] = vec_s[member]

    def vector_step(step):
        if step == 0:
            group_all(*vector_1).wait_recv()
            vecz_r[z] = sum(vec_r[j] for j in range(GROUP))
            for peer in axis_peers("z"):
                along(*vector_z, peer).start()
        elif step == 1:
            along_all(*vector_z).wait_recv()
            vecy_r[y] = sum(vecz_r[j] for j in range(NZ))
            for peer in axis_peers("y"):
                along(*vector_y, peer).start()
        elif step == 2:
            along_all(*vector_y).wait_recv()
            veco_r[member] = sum(vecy_r[j] for j in range(NY))
            for peer in group_peers():
                vector_copy(peer).start()
        else:
            group_all(*vector_2).wait_recv()
            for j in range(GROUP):
                for position in range(3):
                    for h in range(2):
                        for b in range(2):
                            lanes = pl.ds((2 * j + b) * BW + h * HALF, HALF)
                            line = veco_r[j, pl.ds(position * 4 + h * 2 + b, 1), :]
                            if position < 2:
                                bg_ref[pl.ds(position, 1), lanes] = line
                            else:
                                rg_ref[:, lanes] = line

    pl.semaphore_wait(barrier, (GROUP - 1) + (NZ - 1) + (NY - 1))
    local_turns(0, 0, NX - 1)
    last_turn(0)
    local_turns(1, 0, 1)
    to_z(0)
    local_turns(1, 1, NX - 1)
    last_turn(1)
    factors(0)
    to_z(1)
    factors(1)
    to_y(0)
    to_members(0)
    to_y(1)
    entered(0)
    to_members(1)
    for high in range(2):
        gradients(0, high)
    for high in range(2):
        core_sum(0, high)
    for part in range(len(PARTS[0])):
        far_start(0, part, 0)
    entered(1)
    soon = lax.rem(y, 2)
    gradients(1, soon)
    gradients(1, 1 - soon)
    core_sum(1, soon)
    for part, (_, _, order) in enumerate(PARTS[1]):
        if order[0] == "y":
            far_start(1, part, 0)
    vector_out()
    core_sum(1, 1 - soon)
    for part, (_, _, order) in enumerate(PARTS[1]):
        if order[0] != "y":
            far_start(1, part, 0)
    for event in EVENTS:
        if isinstance(event, str):
            kind, number = event.split()
            (through if kind == "through" else vector_step)(int(number))
            continue
        h, part, number = event
        far_finish(h, part, number)
        if number + 1 < len(rounds_of(PARTS[h][part][2])):
            far_start(h, part, number + 1)
    for h in range(2):
        gg_ref[:, pl.ds(h * HALF, HALF)] = part_v[h, y // 2, lax.rem(y, 2), z, x]

    summaries_sent()
    group_all(*vector_1).wait_send()
    group_all(*vector_2).wait_send()
    along_all(*vector_z).wait_send()
    along_all(*vector_y).wait_send()
    for h, part, number in LANDING:
        far_all(h, part, number).wait_send()
    for h in range(2):
        for high in range(2):
            core_all(h, high).wait_send()
    pltpu.make_async_copy(out_v, out_v, out_sem).wait()


def finish(*refs):
    sources, results, held, sem = refs[:4], refs[4:8], refs[8:12], refs[12]
    count = 0
    pairs = []
    for source, result, hold in zip(sources, results, held):
        rows = source.shape[0]
        size = 16 if rows == ROWS else rows
        for top in range(0, rows, size):
            at = pl.ds(top, size)
            pairs.append((
                pltpu.make_async_copy(source.at[at], hold.at[at], sem.at[0, count]),
                pltpu.make_async_copy(hold.at[at], result.at[at], sem.at[1, count]),
            ))
            count += 1
    for into, _ in pairs:
        into.start()
    for into, out in pairs:
        into.wait()
        out.start()
    for _, out in pairs:
        out.wait()


def per_device(inputs, grad_out, gate_weights, gate_biases, decay_rate):
    shape = inputs.shape
    hbm = pl.BlockSpec(memory_space=pl.ANY)
    vmem = pl.BlockSpec(memory_space=pltpu.VMEM)
    dma = pltpu.SemaphoreType.DMA
    block32 = pltpu.VMEM((2, PAIRS, ROWS, BW), F32)
    block16 = pltpu.VMEM((BLOCKS, ROWS, BW), BF16)
    unit32 = pltpu.VMEM((2, ROWS, BW), F32)
    scratch = [
        block16, block16, pltpu.VMEM((2, BLOCKS, BW, BW), BF16),
        pltpu.VMEM((2, D), F32), pltpu.VMEM((1, D), F32), block16,
        pltpu.VMEM((3, ROWS, 2 * ROWS), BF16), pltpu.VMEM((2, 2, ROWS, BW), F32),
        unit32, unit32, pltpu.VMEM((2, 3, 2 * ROWS, BW), BF16),
        block32, pltpu.VMEM((BLOCKS, 2, ROWS, BW), BF16),
    ]
    scratch += [block32] * 9
    scratch += [
        pltpu.VMEM((2, GROUP, 16, 128), F32), pltpu.VMEM((2, GROUP, 16, 128), F32),
        pltpu.VMEM((2, NZ, 16, 128), F32), pltpu.VMEM((2, NY, 16, 128), F32),
        pltpu.VMEM((2, GROUP, 8, 128), F32), pltpu.VMEM((2, GROUP, 8, 128), F32),
        pltpu.VMEM((GROUP, 16, 128), F32), pltpu.VMEM((GROUP, 16, 128), F32),
        pltpu.VMEM((NZ, 16, 128), F32), pltpu.VMEM((NY, 16, 128), F32),
        pltpu.VMEM((GROUP, 16, 128), F32),
        pltpu.VMEM((2, 2, 2, NZ, NX, NC, 32, HALF), F32),
        pltpu.VMEM((2, 2, 2, NZ, NX, 32, HALF), F32),
        dma((3, 4)), dma((2,)), dma(()),
        dma((2,)), dma((2,)), dma((2,)), dma((2,)), dma((2,)), dma((2,)), dma((2,)), dma((2,)),
        dma(()), dma(()), dma(()), dma(()), dma(()), dma(()), dma(()), dma(()),
        dma((2, 2)), dma((2, 2)), dma((len(LANDING),)), dma((len(LANDING),)),
    ]
    scratch += [pltpu.VMEM(found, F32) for found in LANDING_SHAPES]
    shapes = (
        jax.ShapeDtypeStruct((ROWS, D), BF16),
        jax.ShapeDtypeStruct((32, BW), F32),
        jax.ShapeDtypeStruct((2, D), F32),
        jax.ShapeDtypeStruct((1, D), F32),
    )
    results = pl.pallas_call(
        kernel,
        out_shape=shapes,
        in_specs=[hbm] * 5,
        out_specs=(hbm, vmem, vmem, vmem),
        scratch_shapes=scratch,
        compiler_params=pltpu.CompilerParams(
            collective_id=0, has_side_effects=True, vmem_limit_bytes=60 * 2**20
        ),
    )(
        inputs.reshape(ROWS, D), grad_out.reshape(ROWS, D), gate_weights,
        gate_biases, decay_rate.reshape(1, D),
    )
    input_grad, gate_grads, bias_grads, rate_grad = pl.pallas_call(
        finish, out_shape=shapes, in_specs=[hbm] * 4, out_specs=[hbm] * 4,
        scratch_shapes=[pltpu.VMEM(found.shape, found.dtype) for found in shapes] + [dma((2, 11))],
    )(*results)
    return (input_grad.reshape(shape), gate_grads, bias_grads, rate_grad.reshape(D))


def solution(mesh):
    in_specs = (P(None, ("outer", "inner"), None), P(None, ("outer", "inner"), None), P(), P(), P())
    out_specs = (P(None, ("outer", "inner"), None), P(("outer", "inner"), None), P(), P())
    return jax.shard_map(
        per_device, mesh=mesh, in_specs=in_specs, out_specs=out_specs, check_vma=False
    )
```

```python
import functools

import jax
import jax.numpy as jnp
from jax import lax
from jax.experimental import pallas as pl
from jax.experimental.pallas import tpu as pltpu
from jax.sharding import PartitionSpec as P

F32, BF16 = jnp.float32, jnp.bfloat16
rate_gain = 8.0
NY, NZ, NX, NC = 4, 8, 4, 2
GROUP = NX * NC
BLOCKS, BW, D = 16, 256, 4096
SEQS, STEPS = 2, 64
ROWS = SEQS * STEPS
PAIRS = BLOCKS // 2
SLAB = 32
SIZES = {"y": NY, "z": NZ, "x": NX}

HALF = BW // 2

PARTS = (
    ((0, 16, "zyx"), (16, 8, "zxy"), (24, 8, "yxz")),
    ((0, 16, "xyz"), (16, 8, "yxz"), (24, 8, "yxz")),
)


def rounds_of(order):
    rounds = []
    for stage, axis in enumerate(order):
        if stage == 0:
            rounds += [(stage, axis, step) for step in range(1, SIZES[axis] // 2 + 1)]
        else:
            rounds.append((stage, axis, 0))
    return rounds


def free_axes(order, stage):
    return [axis for axis in "yzx" if axis in order[stage + 1 :]]


def lead_shape(axes, halved):
    shape = []
    for position, axis in enumerate(axes):
        half = halved and position == 0
        if axis == "y":
            shape += [1 if half else 2, 2]
        else:
            shape += [SIZES[axis] // 2 if half else SIZES[axis]]
    return tuple(shape)


def landing_buffers():
    places, shapes = {}, []
    for h in range(2):
        for part, (_, rows, order) in enumerate(PARTS[h]):
            for number, (stage, axis, step) in enumerate(rounds_of(order)):
                count = SIZES[axis] if step == 0 else 2
                places[h, part, number] = len(shapes)
                lead = lead_shape(free_axes(order, stage), step == 1)
                shapes.append((count,) + lead + (rows, HALF))
    return places, shapes


LANDING, LANDING_SHAPES = landing_buffers()

EVENTS = [
    (0, 0, 0), (0, 2, 0), (0, 1, 0), "through 0", "through 1", "through 2", (0, 0, 1), (0, 2, 1),
    "vector 0", (0, 1, 1), (1, 0, 0), (1, 1, 0), (1, 2, 0), "through 3", (0, 2, 2), (0, 0, 2),
    "vector 1", (0, 1, 2), (1, 1, 1), (1, 0, 1), (1, 2, 1), "vector 2", (0, 2, 3), (0, 0, 3),
    (1, 1, 2), (0, 1, 3), "vector 3", (1, 2, 2), (1, 0, 2), (0, 0, 4), (0, 1, 4), (1, 1, 3),
    (1, 2, 3), (0, 0, 5), (0, 1, 5), (1, 0, 3),
]


def kernel(
    x_hbm, go_hbm, w_hbm, bias_hbm, rate_hbm,
    out_hbm, gg_ref, bg_ref, rg_ref,
    x_v, go_v, w_v, bias_v, rate_v, out_v,
    tri_v, pre_v, drive_v, lc_v, split_v, dg_v, p_v,
    inv_v, cum_v, before_v, tail_v, c_v, e_v, f_v, q3_v, q4_v,
    sum_s, sum_r, zsum_r, ysum_r, ent_s, ent_r,
    vec_s, vec_r, vecz_r, vecy_r, veco_r,
    grad_v, part_v,
    in_sem, small_sem, out_sem,
    g1_send, g1_recv, z1_send, z1_recv, y1_send, y1_recv, g2_send, g2_recv,
    v1_send, v1_recv, vz_send, vz_recv, vy_send, vy_recv, v2_send, v2_recv,
    core_send, core_recv, far_send, far_recv,
    *landing,
):
    y = lax.axis_index("outer")
    inner = lax.axis_index("inner")
    z = inner // GROUP
    member = lax.rem(inner, GROUP)
    x = member // NC
    core = lax.rem(member, NC)

    def device(y_at, z_at, member_at):
        return (y_at, z_at * GROUP + member_at)

    barrier = pltpu.get_barrier_semaphore()

    def greet(target):
        pl.semaphore_signal(barrier, inc=1, device_id=target, device_id_type=pl.DeviceIdType.MESH)

    for step in range(1, GROUP):
        greet(device(y, z, lax.rem(member + step, GROUP)))
    for step in range(1, NZ):
        greet(device(y, lax.rem(z + step, NZ), member))
    for step in range(1, NY):
        greet(device(lax.rem(y + step, NY), z, member))

    def chip_at(turn):
        return lax.rem(x + 1 + turn, NX)

    def start_loads(turn, carry):
        step = chip_at(turn)
        blocks = pl.ds(4 * step, 4)
        for b in range(4):
            k = 4 * step + b
            lanes = pl.ds(pl.multiple_of(k * BW, BW), BW)
            pltpu.make_async_copy(x_hbm.at[:, lanes], x_v.at[k], in_sem.at[0, step]).start()
        pltpu.make_async_copy(w_hbm.at[:, blocks], w_v.at[:, blocks], in_sem.at[1, step]).start()
        for b in range(4):
            k = 4 * step + b
            lanes = pl.ds(pl.multiple_of(k * BW, BW), BW)
            pltpu.make_async_copy(go_hbm.at[:, lanes], go_v.at[k], in_sem.at[2, step]).start()
        return carry

    def wait_loads(step):
        blocks = pl.ds(4 * step, 4)
        pltpu.make_async_copy(x_v.at[blocks], x_v.at[blocks], in_sem.at[0, step]).wait()
        pltpu.make_async_copy(w_hbm.at[:, blocks], w_v.at[:, blocks], in_sem.at[1, step]).wait()
        pltpu.make_async_copy(go_v.at[blocks], go_v.at[blocks], in_sem.at[2, step]).wait()

    bias_copy = pltpu.make_async_copy(bias_hbm, bias_v, small_sem.at[0])
    rate_copy = pltpu.make_async_copy(rate_hbm, rate_v, small_sem.at[1])
    bias_copy.start()
    rate_copy.start()
    lax.fori_loop(0, 4, start_loads, 0)

    row = lax.broadcasted_iota(jnp.int32, (ROWS, 2 * ROWS), 0)
    col = lax.broadcasted_iota(jnp.int32, (ROWS, 2 * ROWS), 1)
    col = jnp.where(col >= ROWS, col - ROWS, col)
    same = jnp.where(row >= STEPS, 1, 0) == jnp.where(col >= STEPS, 1, 0)
    tri_v[0] = jnp.where(same & (col <= row), 1.0, 0.0).astype(BF16)
    tri_v[1] = jnp.where(same & (col < row), 1.0, 0.0).astype(BF16)
    tri_v[2] = jnp.where(same & (col >= row), 1.0, 0.0).astype(BF16)

    vec_s[...] = jnp.zeros_like(vec_s)
    sum_s[...] = jnp.zeros_like(sum_s)
    bias_copy.wait()
    rate_copy.wait()

    def slabs():
        for b in range(2):
            for top in range(0, ROWS, SLAB):
                yield b, pl.ds(top, SLAB), pl.ds(b * HALF, HALF)

    def split_store(u, which, top, lanes, value):
        high = value.astype(BF16)
        split_v[u, which, pl.ds(top, SLAB), lanes] = high
        split_v[u, which, pl.ds(ROWS + top, SLAB), lanes] = (value - high.astype(F32)).astype(BF16)

    def gate_columns(k, h):
        lanes = pl.ds(h * HALF, HALF)
        return jnp.concatenate([w_v[0, k, :, lanes], w_v[1, k, :, lanes]], axis=1)

    def local(h, step):
        mine = pl.ds(h * HALF, HALF)
        units = [2 * step, 2 * step + 1]
        if h == 0:
            wait_loads(step)
        for u, m in enumerate(units):
            for b in range(2):
                k = 2 * m + b
                pre_v[u, b] = jnp.dot(x_v[k], gate_columns(k, h), preferred_element_type=F32)
        for u, m in enumerate(units):
            for b, rows, lanes in slabs():
                k = 2 * m + b
                column = pl.ds(pl.multiple_of(k * BW + h * HALF, HALF), HALF)
                rate = rate_v[0:1, column]
                pre_r = pre_v[u, b, rows, pl.ds(0, HALF)] + bias_v[0:1, column]
                pre_i = pre_v[u, b, rows, pl.ds(HALF, HALF)] + bias_v[1:2, column]
                recur = 1.0 / (1.0 + jnp.exp(-pre_r))
                inject = 1.0 / (1.0 + jnp.exp(-pre_i))
                values = x_v[k, rows, mine].astype(F32)
                log_decay = (-rate_gain * rate) * recur
                decay = jnp.exp(log_decay)
                series = -log_decay * (
                    1.0 + log_decay * (0.5 + log_decay * (1.0 / 6.0 + log_decay * (1.0 / 24.0)))
                )
                lost = jnp.where(log_decay > -0.1, series, 1.0 - decay)
                square = lost * (1.0 + decay)
                inverse_scale = lax.rsqrt(square)
                scale = square * inverse_scale
                driven = inject * values
                drive_v[u, rows, lanes] = scale * driven
                split_store(u, 0, rows.start, lanes, log_decay)
                at = (h, m, rows, lanes)
                e_v[at], c_v[at], f_v[at] = decay, inverse_scale, recur
                q4_v[at], q3_v[at] = scale, inject
        for u, m in enumerate(units):
            lc_v[u] = jnp.dot(tri_v[0], split_v[u, 0], preferred_element_type=F32)
        for u, m in enumerate(units):
            for b, rows, lanes in slabs():
                log_cum = lc_v[u, rows, lanes]
                cum = jnp.exp(log_cum)
                inverse = jnp.exp(-log_cum)
                inv_v[h, m, rows, lanes] = inverse
                cum_v[h, m, rows, lanes] = cum
                scaled = drive_v[u, rows, lanes] * inverse
                split_store(u, 1, rows.start, lanes, scaled)
                upstream = go_v[2 * m + b, rows, mine].astype(F32)
                split_store(u, 2, rows.start, lanes, cum * upstream)
                last = rows.start + SLAB
                if last % STEPS == 0:
                    slot = (last // STEPS - 1) * 2 + b
                    sum_s[h, m, pl.ds(slot, 1), :] = cum[SLAB - 1 : SLAB]
                    sum_s[h, m, pl.ds(4 + slot, 1), :] = scaled[SLAB - 1 : SLAB]
        for u, m in enumerate(units):
            before_v[h, m] = jnp.dot(tri_v[1], split_v[u, 1], preferred_element_type=F32)
            tail_v[h, m] = jnp.dot(tri_v[2], split_v[u, 2], preferred_element_type=F32)
        for u, m in enumerate(units):
            for s in range(SEQS):
                for b in range(2):
                    slot = s * 2 + b
                    lanes = pl.ds(b * HALF, HALF)
                    before = before_v[h, m, pl.ds(s * STEPS + STEPS - 1, 1), lanes]
                    end = sum_s[h, m, pl.ds(slot, 1), :]
                    held = sum_s[h, m, pl.ds(4 + slot, 1), :]
                    sum_s[h, m, pl.ds(4 + slot, 1), :] = end * (before + held)
                    sum_s[h, m, pl.ds(8 + slot, 1), :] = tail_v[h, m, pl.ds(s * STEPS, 1), lanes]

    def factors(h):
        def body(m, carry):
            for b, rows, lanes in slabs():
                k = 2 * m + b
                at = (h, m, rows, lanes)
                rate = rate_v[0:1, pl.ds(pl.multiple_of(k * BW + h * HALF, HALF), HALF)]
                values = x_v[k, rows, pl.ds(h * HALF, HALF)].astype(F32)
                recur, inject, decay = f_v[at], q3_v[at], e_v[at]
                e = rate_gain * recur
                e_v[at] = e
                c_v[at] = e * (decay * decay) * (inject * values) * c_v[at]
                f_v[at] = rate * (1.0 - recur)
                q4 = q4_v[at] * inject
                q4_v[at] = q4
                q3_v[at] = q4 * values * (1.0 - inject)
            return carry

        lax.fori_loop(0, PAIRS, body, 0)

    def remote(src, dst, send, recv, target):
        return pltpu.make_async_remote_copy(
            src_ref=src, dst_ref=dst, send_sem=send, recv_sem=recv,
            device_id=target, device_id_type=pl.DeviceIdType.MESH,
        )

    def in_group(source, landing, send, recv, peer):
        return remote(source.at[peer], landing.at[member], send, recv, device(y, z, peer))

    def along(axis, landing, send, recv, peer):
        here = z if axis == "z" else y
        target = device(y, peer, member) if axis == "z" else device(peer, z, member)
        return remote(landing.at[here], landing.at[here], send, recv, target)

    def all_of(landing, send, recv, count):
        every = landing.at[pl.ds(0, count - 1)]
        return remote(every, every, send, recv, device(y, z, x * NC + (1 - core)))

    def group_all(source, landing, send, recv):
        return all_of(landing, send, recv, GROUP)

    def along_all(axis, landing, send, recv):
        return all_of(landing, send, recv, SIZES[axis])

    def far_first(size):
        return sorted(range(1, size), key=lambda step: -min(step, size - step))

    def group_peers():
        return [lax.rem(member + step, GROUP) for step in far_first(GROUP)]

    def axis_peers(axis):
        here, size = (z, NZ) if axis == "z" else (y, NY)
        return [lax.rem(here + step, size) for step in far_first(size)]

    mult, first, back = pl.ds(0, 4), pl.ds(4, 4), pl.ds(8, 4)
    ones, zeros = jnp.ones((4, 128), F32), jnp.zeros((4, 128), F32)

    def total_of(ref, count):
        decay = ref[0, mult]
        state = ref[0, first]
        for j in range(1, count):
            state = ref[j, mult] * state + ref[j, first]
            decay = decay * ref[j, mult]
        adjoint = ref[count - 1, back]
        for j in range(count - 2, -1, -1):
            adjoint = ref[j, mult] * adjoint + ref[j, back]
        return decay, state, adjoint

    def put(ref, index, values):
        for position, value in enumerate(values):
            ref[index, pl.ds(4 * position, 4)] = value
        ref[index, pl.ds(12, 4)] = zeros

    def earlier(ref, count, position, decay, state):
        for j in range(count):
            use = j < position
            state = jnp.where(use, ref[j, mult] * state + ref[j, first], state)
            decay = jnp.where(use, ref[j, mult] * decay, decay)
        return decay, state

    def later(ref, count, position, decay, adjoint):
        for j in range(count - 1, -1, -1):
            use = j > position
            adjoint = jnp.where(use, ref[j, mult] * adjoint + ref[j, back], adjoint)
            decay = jnp.where(use, ref[j, mult] * decay, decay)
        return decay, adjoint

    def group_1(h):
        return sum_s.at[h], sum_r.at[h], g1_send.at[h], g1_recv.at[h]

    def group_2(h):
        return ent_s.at[h], ent_r.at[h], g2_send.at[h], g2_recv.at[h]

    def along_z(h):
        return "z", zsum_r.at[h], z1_send.at[h], z1_recv.at[h]

    def along_y(h):
        return "y", ysum_r.at[h], y1_send.at[h], y1_recv.at[h]

    def local_turns(h, start, stop):
        def body(turn, carry):
            chip = chip_at(turn)
            local(h, chip)
            for c in range(NC):
                in_group(*group_1(h), chip * NC + c).start()
            return carry

        lax.fori_loop(start, stop, body, 0)

    def last_turn(h):
        local(h, x)
        in_group(*group_1(h), x * NC + (1 - core)).start()
        sum_r[h, member] = sum_s[h, member]

    def to_z(h):
        group_all(*group_1(h)).wait_recv()
        put(zsum_r.at[h], z, total_of(sum_r.at[h], GROUP))
        for peer in axis_peers("z"):
            along(*along_z(h), peer).start()

    def to_y(h):
        along_all(*along_z(h)).wait_recv()
        put(ysum_r.at[h], y, total_of(zsum_r.at[h], NZ))
        for peer in axis_peers("y"):
            along(*along_y(h), peer).start()

    def to_members(h):
        z_decay, z_state = earlier(zsum_r.at[h], NZ, z, ones, zeros)
        z_fade, z_adjoint = later(zsum_r.at[h], NZ, z, ones, zeros)
        along_all(*along_y(h)).wait_recv()
        state = z_decay * earlier(ysum_r.at[h], NY, y, ones, zeros)[1] + z_state
        adjoint = z_fade * later(ysum_r.at[h], NY, y, ones, zeros)[1] + z_adjoint
        for j in range(GROUP):
            ent_s[h, j, pl.ds(0, 4)] = state
            state = sum_r[h, j, mult] * state + sum_r[h, j, first]
        for j in range(GROUP - 1, -1, -1):
            ent_s[h, j, pl.ds(4, 4)] = adjoint
            adjoint = sum_r[h, j, mult] * adjoint + sum_r[h, j, back]
        for peer in group_peers():
            in_group(*group_2(h), peer).start()
        ent_r[h, member] = ent_s[h, member]

    def entered(h):
        group_all(*group_2(h)).wait_recv()

    def summaries_sent():
        for h in range(2):
            group_all(*group_1(h)).wait_send()
            group_all(*group_2(h)).wait_send()
            along_all(*along_z(h)).wait_send()
            along_all(*along_y(h)).wait_send()

    other = device(y, z, x * NC + (1 - core))

    def batch_of(h, m):
        return lax.rem(m, 4) // 2 if h == 0 else m // 4

    def core_copy(h, m):
        high, low = m // 4, pl.ds(2 * lax.rem(m, 4), 2)
        return remote(
            grad_v.at[h, :, high, low, :, 1 - core], part_v.at[h, :, high, low],
            core_send.at[h, batch_of(h, m)], core_recv.at[h, batch_of(h, m)], other,
        )

    def core_all(h, batch):
        every = part_v.at[h, :, :, pl.ds(4 * batch, 4)] if h == 0 else part_v.at[h, :, batch]
        return remote(every, every, core_send.at[h, batch], core_recv.at[h, batch], other)

    def gradient(h, step):
        units = [2 * step, 2 * step + 1]
        for m in units:
            for b in range(2):
                k = 2 * m + b
                lanes = pl.ds(b * HALF, HALF)
                sums = [jnp.zeros((8, 128), F32) for _ in range(3)]
                for s in range(SEQS):
                    slot = s * 2 + b
                    entering = ent_r[h, m, pl.ds(slot, 1), :]
                    arriving = ent_r[h, m, pl.ds(4 + slot, 1), :] * sum_s[h, m, pl.ds(slot, 1), :]
                    for top in range(s * STEPS, (s + 1) * STEPS, SLAB):
                        rows = pl.ds(top, SLAB)
                        at = (h, m, rows, lanes)
                        adj = inv_v[at] * (tail_v[at] + arriving)
                        carried = cum_v[at] * (before_v[at] + entering)
                        rated = adj * (c_v[at] - carried * e_v[at])
                        pre_r = rated * f_v[at]
                        pre_i = adj * q3_v[at]
                        dg_v[at] = adj * q4_v[at]
                        p_v[k, h, rows, pl.ds(0, HALF)] = pre_r.astype(BF16)
                        p_v[k, h, rows, pl.ds(HALF, HALF)] = pre_i.astype(BF16)
                        for position, value in enumerate((pre_r, pre_i, rated)):
                            for part in range(0, SLAB, 8):
                                sums[position] = sums[position] + value[part : part + 8]
                for position in range(3):
                    line = position * 4 + h * 2 + b
                    vec_s[m, pl.ds(line, 1), :] = jnp.sum(sums[position], axis=0, keepdims=True)
        for m in units:
            for b in range(2):
                k = 2 * m + b
                outer = lax.dot_general(
                    x_v[k], p_v[k, h], (((0,), (0,)), ((), ())), preferred_element_type=F32
                )
                for g in range(2):
                    grad_v[h, g, m // 4, 2 * lax.rem(m, 4) + b] = outer[
                        :, g * HALF : (g + 1) * HALF
                    ].reshape(NX, NC, 32, HALF)
            core_copy(h, m).start()

    def gradients(h, batch):
        def body(step, carry):
            gradient(h, batch + 2 * step if h == 0 else 2 * batch + step)
            return carry

        lax.fori_loop(0, 2, body, 0)

    def out_copy(k):
        lanes = pl.ds(pl.multiple_of(k * BW, BW), BW)
        return pltpu.make_async_copy(out_v.at[k], out_hbm.at[:, lanes], out_sem)

    def through(quarter):
        def body(m, carry):
            for b in range(2):
                k = 2 * m + b
                across = (((1,), (1,)), ((), ()))
                for h in range(2):
                    back_in = lax.dot_general(
                        p_v[k, h], gate_columns(k, h), across, preferred_element_type=F32
                    )
                    total = back_in if h == 0 else total + back_in
                for h in range(2):
                    mine = pl.ds(h * HALF, HALF)
                    direct = dg_v[h, m, :, pl.ds(b * HALF, HALF)]
                    out_v[k, :, mine] = (direct + total[:, h * HALF : (h + 1) * HALF]).astype(BF16)
                out_copy(k).start()
            return carry

        lax.fori_loop(2 * quarter, 2 * quarter + 2, body, 0)

    def core_sum(h, batch):
        core_all(h, batch).wait_recv()

        def body(i, carry):
            high, at = (i // 4, 4 * batch + lax.rem(i, 4)) if h == 0 else (batch, i)
            for g in range(2):
                part_v[h, g, high, at] = part_v[h, g, high, at] + grad_v[h, g, high, at, :, core]
            return carry

        lax.fori_loop(0, 8, body, 0)

    here = {"y": y, "z": z, "x": x}

    def index_of(axis, at, whole, halved, side):
        if not whole:
            return (at // 2, lax.rem(at, 2)) if axis == "y" else (at,)
        if axis == "y":
            return (pl.ds(side, 1) if halved else pl.ds(0, 2), pl.ds(0, 2))
        size = SIZES[axis]
        return (pl.ds(side * (size // 2), size // 2) if halved else pl.ds(0, size),)

    def view(h, part, stage, target, halved, side):
        row0, rows, order = PARTS[h][part]
        axis, axes = order[stage], free_axes(order, stage)
        found = (h,)
        for name in "yzx":
            if name == axis:
                found += index_of(name, target, False, False, 0)
            elif name in axes:
                found += index_of(name, 0, True, halved and name == axes[0], side)
            else:
                found += index_of(name, here[name], False, False, 0)
        return found + (pl.ds(row0, rows), slice(None))

    def far_all(h, part, number):
        buffer = landing[LANDING[h, part, number]]
        axis, step = rounds_of(PARTS[h][part][2])[number][1:]
        every = buffer if step > 0 else buffer.at[pl.ds(0, SIZES[axis] - 1)]
        at = LANDING[h, part, number]
        return remote(every, every, far_send.at[at], far_recv.at[at], other)

    def ring_copy(h, part, number, side):
        stage, axis, step = rounds_of(PARTS[h][part][2])[number]
        size = SIZES[axis]
        half = size // 2
        sent = here[axis] + (half - step + 1 if side == 0 else size - half + step - 1)
        place = dict(here)
        place[axis] = lax.rem(here[axis] + (1 if side == 0 else size - 1), size)
        at = LANDING[h, part, number]
        return remote(
            part_v.at[view(h, part, stage, lax.rem(sent, size), step == 1, side)],
            landing[LANDING[h, part, number]].at[side], far_send.at[at], far_recv.at[at],
            device(place["y"], place["z"], place["x"] * NC + core),
        )

    def direct_copy(h, part, number, peer):
        stage, axis, _ = rounds_of(PARTS[h][part][2])[number]
        place = dict(here)
        place[axis] = peer
        at = LANDING[h, part, number]
        return remote(
            part_v.at[view(h, part, stage, peer, False, 0)],
            landing[LANDING[h, part, number]].at[here[axis]], far_send.at[at], far_recv.at[at],
            device(place["y"], place["z"], place["x"] * NC + core),
        )

    def copies_out(h, part, number):
        _, axis, step = rounds_of(PARTS[h][part][2])[number]
        if step > 0:
            return [ring_copy(h, part, number, side) for side in range(2)]
        peers = [lax.rem(here[axis] + far, SIZES[axis]) for far in far_first(SIZES[axis])]
        return [direct_copy(h, part, number, peer) for peer in peers]

    def far_start(h, part, number):
        for copy in copies_out(h, part, number):
            copy.start()

    def add_landed(at, axes, halved, side, buffer, slots):
        if len(axes) == 0:
            part_v[at] = part_v[at] + sum(buffer[slot] for slot in slots)
            return
        axis = axes[0]
        size = SIZES[axis] // 2 if halved else SIZES[axis]
        position = 1 + {"y": 0, "z": 2, "x": 3}[axis]
        width = 2 if axis == "y" else 1
        base = size * side if halved else 0

        def body(i, carry):
            if axis == "y":
                from_, to = (i // 2, lax.rem(i, 2)), ((base + i) // 2, lax.rem(base + i, 2))
            else:
                from_, to = (i,), (base + i,)
            place = at[:position] + to + at[position + width :]
            part_v[place] = part_v[place] + sum(buffer[(slot,) + from_] for slot in slots)
            return carry

        lax.fori_loop(0, size, body, 0)

    def far_finish(h, part, number):
        order = PARTS[h][part][2]
        stage, axis, step = rounds_of(order)[number]
        size, axes = SIZES[axis], free_axes(order, stage)
        buffer = landing[LANDING[h, part, number]]
        far_all(h, part, number).wait_recv()
        if step == 0:
            peers = [lax.rem(here[axis] + far, size) for far in range(1, size)]
            at = view(h, part, stage, here[axis], False, 0)
            add_landed(at, axes, False, 0, buffer, peers)
            return
        half = size // 2
        for side in range(2):
            came = here[axis] + (half - step if side == 0 else size - half + step)
            at = view(h, part, stage, lax.rem(came, size), step == 1, side)
            add_landed(at, axes, step == 1, side, buffer, [side])

    vector_1 = (vec_s, vec_r, v1_send, v1_recv)
    vector_z = ("z", vecz_r, vz_send, vz_recv)
    vector_y = ("y", vecy_r, vy_send, vy_recv)

    vector_2 = (veco_r, veco_r, v2_send, v2_recv)

    def vector_copy(peer):
        return remote(veco_r.at[member], veco_r.at[member], v2_send, v2_recv, device(y, z, peer))

    def vector_out():
        for peer in group_peers():
            in_group(*vector_1, peer).start()
        vec_r[member] = vec_s[member]

    def vector_step(step):
        if step == 0:
            group_all(*vector_1).wait_recv()
            vecz_r[z] = sum(vec_r[j] for j in range(GROUP))
            for peer in axis_peers("z"):
                along(*vector_z, peer).start()
        elif step == 1:
            along_all(*vector_z).wait_recv()
            vecy_r[y] = sum(vecz_r[j] for j in range(NZ))
            for peer in axis_peers("y"):
                along(*vector_y, peer).start()
        elif step == 2:
            along_all(*vector_y).wait_recv()
            veco_r[member] = sum(vecy_r[j] for j in range(NY))
            for peer in group_peers():
                vector_copy(peer).start()
        else:
            group_all(*vector_2).wait_recv()
            for j in range(GROUP):
                for position in range(3):
                    for h in range(2):
                        for b in range(2):
                            lanes = pl.ds((2 * j + b) * BW + h * HALF, HALF)
                            line = veco_r[j, pl.ds(position * 4 + h * 2 + b, 1), :]
                            if position < 2:
                                bg_ref[pl.ds(position, 1), lanes] = line
                            else:
                                rg_ref[:, lanes] = line

    pl.semaphore_wait(barrier, (GROUP - 1) + (NZ - 1) + (NY - 1))
    local_turns(0, 0, NX - 1)
    last_turn(0)
    local_turns(1, 0, 1)
    to_z(0)
    local_turns(1, 1, NX - 1)
    last_turn(1)
    factors(0)
    to_z(1)
    factors(1)
    to_y(0)
    to_members(0)
    to_y(1)
    entered(0)
    to_members(1)
    far_z = 1 - z // 4
    gradients(0, far_z)
    gradients(0, 1 - far_z)
    core_sum(0, far_z)
    for part, (_, _, order) in enumerate(PARTS[0]):
        if order[0] == "z":
            far_start(0, part, 0)
    core_sum(0, 1 - far_z)
    for part, (_, _, order) in enumerate(PARTS[0]):
        if order[0] != "z":
            far_start(0, part, 0)
    entered(1)
    soon = lax.rem(y, 2)
    gradients(1, soon)
    gradients(1, 1 - soon)
    core_sum(1, soon)
    for part, (_, _, order) in enumerate(PARTS[1]):
        if order[0] == "y":
            far_start(1, part, 0)
    vector_out()
    core_sum(1, 1 - soon)
    for part, (_, _, order) in enumerate(PARTS[1]):
        if order[0] != "y":
            far_start(1, part, 0)
    for event in EVENTS:
        if isinstance(event, str):
            kind, number = event.split()
            (through if kind == "through" else vector_step)(int(number))
            continue
        h, part, number = event
        far_finish(h, part, number)
        if number + 1 < len(rounds_of(PARTS[h][part][2])):
            far_start(h, part, number + 1)
    for h in range(2):
        gg_ref[:, pl.ds(h * HALF, HALF)] = part_v[h, y // 2, lax.rem(y, 2), z, x]

    summaries_sent()
    group_all(*vector_1).wait_send()
    group_all(*vector_2).wait_send()
    along_all(*vector_z).wait_send()
    along_all(*vector_y).wait_send()
    for h, part, number in LANDING:
        far_all(h, part, number).wait_send()
    for h in range(2):
        for high in range(2):
            core_all(h, high).wait_send()
    pltpu.make_async_copy(out_v, out_v, out_sem).wait()


def finish(*refs):
    sources, results, held, sem = refs[:4], refs[4:8], refs[8:12], refs[12]
    count = 0
    pairs = []
    for source, result, hold in zip(sources, results, held):
        rows = source.shape[0]
        size = 16 if rows == ROWS else rows
        for top in range(0, rows, size):
            at = pl.ds(top, size)
            pairs.append((
                pltpu.make_async_copy(source.at[at], hold.at[at], sem.at[0, count]),
                pltpu.make_async_copy(hold.at[at], result.at[at], sem.at[1, count]),
            ))
            count += 1
    for into, _ in pairs:
        into.start()
    for into, out in pairs:
        into.wait()
        out.start()
    for _, out in pairs:
        out.wait()


def per_device(inputs, grad_out, gate_weights, gate_biases, decay_rate):
    shape = inputs.shape
    hbm = pl.BlockSpec(memory_space=pl.ANY)
    vmem = pl.BlockSpec(memory_space=pltpu.VMEM)
    dma = pltpu.SemaphoreType.DMA
    block32 = pltpu.VMEM((2, PAIRS, ROWS, BW), F32)
    block16 = pltpu.VMEM((BLOCKS, ROWS, BW), BF16)
    unit32 = pltpu.VMEM((2, ROWS, BW), F32)
    scratch = [
        block16, block16, pltpu.VMEM((2, BLOCKS, BW, BW), BF16),
        pltpu.VMEM((2, D), F32), pltpu.VMEM((1, D), F32), block16,
        pltpu.VMEM((3, ROWS, 2 * ROWS), BF16), pltpu.VMEM((2, 2, ROWS, BW), F32),
        unit32, unit32, pltpu.VMEM((2, 3, 2 * ROWS, BW), BF16),
        block32, pltpu.VMEM((BLOCKS, 2, ROWS, BW), BF16),
    ]
    scratch += [block32] * 9
    scratch += [
        pltpu.VMEM((2, GROUP, 16, 128), F32), pltpu.VMEM((2, GROUP, 16, 128), F32),
        pltpu.VMEM((2, NZ, 16, 128), F32), pltpu.VMEM((2, NY, 16, 128), F32),
        pltpu.VMEM((2, GROUP, 8, 128), F32), pltpu.VMEM((2, GROUP, 8, 128), F32),
        pltpu.VMEM((GROUP, 16, 128), F32), pltpu.VMEM((GROUP, 16, 128), F32),
        pltpu.VMEM((NZ, 16, 128), F32), pltpu.VMEM((NY, 16, 128), F32),
        pltpu.VMEM((GROUP, 16, 128), F32),
        pltpu.VMEM((2, 2, 2, NZ, NX, NC, 32, HALF), F32),
        pltpu.VMEM((2, 2, 2, NZ, NX, 32, HALF), F32),
        dma((3, 4)), dma((2,)), dma(()),
        dma((2,)), dma((2,)), dma((2,)), dma((2,)), dma((2,)), dma((2,)), dma((2,)), dma((2,)),
        dma(()), dma(()), dma(()), dma(()), dma(()), dma(()), dma(()), dma(()),
        dma((2, 2)), dma((2, 2)), dma((len(LANDING),)), dma((len(LANDING),)),
    ]
    scratch += [pltpu.VMEM(found, F32) for found in LANDING_SHAPES]
    shapes = (
        jax.ShapeDtypeStruct((ROWS, D), BF16),
        jax.ShapeDtypeStruct((32, BW), F32),
        jax.ShapeDtypeStruct((2, D), F32),
        jax.ShapeDtypeStruct((1, D), F32),
    )
    results = pl.pallas_call(
        kernel,
        out_shape=shapes,
        in_specs=[hbm] * 5,
        out_specs=(hbm, vmem, vmem, vmem),
        scratch_shapes=scratch,
        compiler_params=pltpu.CompilerParams(
            collective_id=0, has_side_effects=True, vmem_limit_bytes=60 * 2**20
        ),
    )(
        inputs.reshape(ROWS, D), grad_out.reshape(ROWS, D), gate_weights,
        gate_biases, decay_rate.reshape(1, D),
    )
    input_grad, gate_grads, bias_grads, rate_grad = pl.pallas_call(
        finish, out_shape=shapes, in_specs=[hbm] * 4, out_specs=[hbm] * 4,
        scratch_shapes=[pltpu.VMEM(found.shape, found.dtype) for found in shapes] + [dma((2, 11))],
    )(*results)
    return (input_grad.reshape(shape), gate_grads, bias_grads, rate_grad.reshape(D))


def solution(mesh):
    in_specs = (P(None, ("outer", "inner"), None), P(None, ("outer", "inner"), None), P(), P(), P())
    out_specs = (P(None, ("outer", "inner"), None), P(("outer", "inner"), None), P(), P())
    return jax.shard_map(
        per_device, mesh=mesh, in_specs=in_specs, out_specs=out_specs, check_vma=False
    )
```
